256 devices in a mesh: replica: 4 (over x_lo, core), fsdp: 64 (over x_hi, y, z).
Axes of the slice: x: 4 (x_hi: 2, x_lo: 2; x = x_hi * 2 + x_lo), y: 4, z: 8, core: 2. Of those that a mesh axis runs over, the one named last changes fastest.
Arguments:
- hidden_in: bfloat16 [4, 16384, 8192], P('replica', 'fsdp'), may hold values from -27 to 27
- norm_gain: float32 [4, 8192], P('replica'), may hold values from 0.1 to 1.9
- key_weight: bfloat16 [4, 8192, 512], P('replica', 'fsdp'), may hold values from -1 to 1.5
- key_cotangent: bfloat16 [4, 16384, 512], P('replica', 'fsdp'), may hold values from -40 to 40
- outer_params: float32 [8, 8192, 512], P(None, 'fsdp'), may hold values from -6 to 6
- outer_momentum: float32 [8, 8192, 512], P(None, 'fsdp'), may hold values from -3 to 3
- inner_params: float32 [4, 8, 8192, 512], P('replica', None, 'fsdp'), may hold values from -6 to 6
- fragment_index: int32 [1], replicated, may hold values from 0 to 7
Outputs:
- key_out: bfloat16 [4, 16384, 512], P('replica', 'fsdp')
- grad_weight: float32 [4, 8192, 512], P('replica', 'fsdp')
- grad_hidden: bfloat16 [4, 16384, 8192], P('replica', 'fsdp')
- grad_gain: float32 [4, 8192], P('replica')
- new_params: float32 [8192, 512], P('fsdp')
- new_momentum: float32 [8192, 512], P('fsdp')
The draws below stay inside these ranges and needn't reach their ends.
All inputs are finite; a program needn't handle non-finite values.
Results may differ from the reference program's by a relative error of at most 0.0049.
Values may be sent and summed in bfloat16 or wider, within the bound.
No kernel may reach another device: no remote copies, remote signals or barrier semaphores. Data moves between devices by JAX's collectives and lax.ppermute only.
A program may use at most 128 MiB of HBM per device.

```python
import jax
import jax.numpy as jnp
from jax import lax

D = 8192
KV = 512
FRAGS = 8
REPLICAS = 4
GROUP_TOK = 16384
N_REPLICA = 4


def base_hidden(key):
    return jnp.clip(jax.random.normal(key, (REPLICAS, GROUP_TOK, D), jnp.float32), -6.0, 6.0)


def first_picks(subkey):
    return jax.random.permutation(subkey, D)[:KV]


def picked_features(key):
    group_keys = jax.random.split(jax.random.fold_in(key, 5), REPLICAS)
    return jax.vmap(first_picks)(group_keys).astype(jnp.int32)


def pick_columns(rows, columns):
    return rows[:, columns]


def draw_hidden_in(key, part):
    values = base_hidden(key)
    return values.astype(jnp.bfloat16)


def draw_key_weight(key, part):
    chosen = picked_features(key)
    key = jax.random.fold_in(key, 7)
    jitter = jnp.clip(jax.random.normal(key, (REPLICAS, D, KV), jnp.float32), -2.5, 2.5) * D ** (-0.5)
    planted = (jnp.arange(D, dtype=jnp.int32)[None, :, None] == chosen[:, None, :]).astype(jnp.float32)
    return (jitter + 0.75 * planted).astype(jnp.bfloat16)


def draw_key_cotangent(key, part):
    base_values = base_hidden(key)
    chosen = picked_features(key)
    picked = jax.vmap(pick_columns)(base_values, chosen)
    key = jax.random.fold_in(key, 11)
    sign_key, jitter_key = jax.random.split(key)
    token_signs = jnp.where(jax.random.bernoulli(sign_key, 0.5, (REPLICAS, GROUP_TOK, 1)), 1.0, -1.0)
    position = jnp.arange(GROUP_TOK, dtype=jnp.float32) / (GROUP_TOK - 1)
    rising = (1.0 + 2.0 * position)[None, :, None]
    jitter = jnp.clip(jax.random.normal(jitter_key, (REPLICAS, GROUP_TOK, KV), jnp.float32), -6.0, 6.0)
    return (rising * (0.6 * token_signs * picked + 0.25 * jitter)).astype(jnp.bfloat16)


def level_of(stream_key, extent, cuts, low, largest):
    def one(dim, shards_of):
        heights = jax.random.uniform(jax.random.fold_in(jax.random.fold_in(stream_key, 6), dim), (shards_of,), jnp.float32, low / len(cuts), largest / len(cuts))
        return jnp.repeat(jnp.exp(heights), extent[dim] // shards_of).reshape((-1,) + (1,) * (len(extent) - dim - 1))

    factor_of = one(*cuts[0])
    for cut in cuts[1:]:
        factor_of = factor_of * one(*cut)
    return factor_of


def scatter_about(stream_key, extent, spread, reach, cuts=(), held_as=jnp.bfloat16):
    entries = jax.random.normal(stream_key, extent, jnp.float32) * spread
    if len(cuts) > 0:
        entries = level_of(stream_key, extent, cuts, -0.22, 0.18) * entries
    return jnp.clip(entries, min=-reach, max=reach).astype(held_as)


def setup_inputs(seed: int = 0) -> dict:
    arg_keys = jax.random.split(jax.random.key(seed), 9)
    return {
        "hidden_in": draw_hidden_in(jax.random.fold_in(arg_keys[8], 71), 0),
        "norm_gain": jnp.clip(1.0 + 0.18 * jax.random.normal(arg_keys[1], (REPLICAS, D), jnp.float32), 0.1, 1.9),
        "key_weight": draw_key_weight(jax.random.fold_in(arg_keys[8], 71), 0),
        "key_cotangent": draw_key_cotangent(jax.random.fold_in(arg_keys[8], 71), 0),
        "outer_params": scatter_about(arg_keys[4], (FRAGS, D, KV), 1.0, 6.0, ((1, 64),), jnp.float32),
        "outer_momentum": scatter_about(arg_keys[5], (FRAGS, D, KV), 0.5, 3.0, ((1, 64),), jnp.float32),
        "inner_params": scatter_about(arg_keys[6], (REPLICAS, FRAGS, D, KV), 1.0, 6.0, ((0, 4), (2, 64)), jnp.float32),
        "fragment_index": jax.random.randint(arg_keys[7], (1,), 0, FRAGS).astype(jnp.int32),
    }


def one_group(hidden, gain_row, weight, cotangent):
    widened = hidden.astype(jnp.float32)
    inverse = lax.rsqrt(lax.optimization_barrier(jnp.mean(widened * widened, axis=-1, keepdims=True)) + 1e-05)
    normed = widened * inverse
    scaled = (normed * gain_row[None, :]).astype(jnp.bfloat16)
    key_out = jnp.dot(scaled, weight, preferred_element_type=jnp.float32).astype(jnp.bfloat16)
    grad_normed = lax.dot_general(cotangent, weight, (((1,), (1,)), ((), ())), preferred_element_type=jnp.float32)
    factor = GROUP_TOK ** (-0.5)
    grad_weight = lax.dot_general(scaled, cotangent, (((0,), (0,)), ((), ())), preferred_element_type=jnp.float32) * factor
    grad_gain = lax.optimization_barrier(jnp.sum(grad_normed * normed, axis=0)) * factor
    weighted = grad_normed * gain_row[None, :]
    inner_mean = lax.optimization_barrier(jnp.mean(weighted * normed, axis=-1, keepdims=True))
    grad_hidden = (inverse * (weighted - normed * inner_mean)).astype(jnp.bfloat16)
    return (key_out, grad_weight, grad_hidden, grad_gain)

def outer_step(current, moment, average):
    moment_new = 0.9 * moment + average
    return (current - 0.7 * (average + 0.9 * moment_new), moment_new)

def reference(hidden_in, norm_gain, key_weight, key_cotangent, outer_params, outer_momentum, inner_params, fragment_index):
    results = [one_group(hidden_in[group], norm_gain[group], key_weight[group], key_cotangent[group]) for group in range(REPLICAS)]
    key_out = jnp.stack([item[0] for item in results])
    grad_weight = jnp.stack([item[1] for item in results])
    grad_hidden = jnp.stack([item[2] for item in results])
    grad_gain = jnp.stack([item[3] for item in results])
    chosen = fragment_index[0].astype(jnp.int32)
    current = lax.dynamic_index_in_dim(outer_params, chosen, 0, keepdims=False)
    moment = lax.dynamic_index_in_dim(outer_momentum, chosen, 0, keepdims=False)
    inner_now = lax.dynamic_index_in_dim(inner_params, chosen, 1, keepdims=False)
    pseudo_grad = current[None] - inner_now
    average = lax.optimization_barrier(jnp.sum(pseudo_grad, axis=0)) / N_REPLICA
    new_params, new_momentum = outer_step(current, moment, average)
    return (key_out, grad_weight, grad_hidden, grad_gain, new_params, new_momentum)
```

```python
import jax
import jax.numpy as jnp
from jax import lax
from jax.sharding import Mesh
from jax.sharding import PartitionSpec as P

GROUP = ("xh", "y", "z")
REPL = ("xl", "core")
SIZE = {"xh": 2, "y": 4, "z": 8}
BF16 = jnp.bfloat16
F32 = jnp.float32


def shift(value, axis, step):
    n = SIZE[axis]
    return lax.ppermute(value, axis, [(i, (i + step) % n) for i in range(n)])


def place(buffer, block, axis, dim, step):
    at = (lax.axis_index(axis) - step) & (SIZE[axis] - 1)
    return lax.dynamic_update_slice_in_dim(buffer, block, at, dim)


def gather(buffer, own, axis, dim, rows):
    n = SIZE[axis]
    buffer = place(buffer, own, axis, dim, 0)
    right = left = own
    for hop in range(1, n // 2):
        right, left = shift(right, axis, 1), shift(left, axis, -1)
        buffer = place(buffer, right, axis, dim, hop)
        buffer = place(buffer, left, axis, dim, -hop)
    half = own.shape[rows] // 2
    low = shift(lax.slice_in_dim(right, 0, half, axis=rows), axis, 1)
    high = shift(lax.slice_in_dim(left, half, 2 * half, axis=rows), axis, -1)
    last = lax.concatenate([low, high], rows)
    return place(buffer, last, axis, dim, n // 2)


def scatter_sum(part, axis, dim, rows):
    n = SIZE[axis]

    def term(step):
        at = (lax.axis_index(axis) + step) & (n - 1)
        return lax.dynamic_slice_in_dim(part, at, 1, dim)

    far = term(n // 2)
    half = far.shape[rows] // 2
    right = shift(lax.slice_in_dim(far, 0, half, axis=rows).astype(BF16), axis, 1)
    left = shift(lax.slice_in_dim(far, half, 2 * half, axis=rows).astype(BF16), axis, -1)
    for hop in range(n // 2 - 1, 0, -1):
        ahead, behind = term(hop), term(-hop)
        if hop == n // 2 - 1:
            low = lax.slice_in_dim(ahead, 0, half, axis=rows) + right.astype(F32)
            ahead = lax.concatenate([low, lax.slice_in_dim(ahead, half, 2 * half, axis=rows)], rows)
            high = lax.slice_in_dim(behind, half, 2 * half, axis=rows) + left.astype(F32)
            behind = lax.concatenate([lax.slice_in_dim(behind, 0, half, axis=rows), high], rows)
        else:
            ahead = ahead + right.astype(F32)
            behind = behind + left.astype(F32)
        right = shift(ahead.astype(BF16), axis, 1)
        left = shift(behind.astype(BF16), axis, -1)
    return term(0) + right.astype(F32) + left.astype(F32)


def swap_sum(part, dim):
    me = lax.axis_index("xh")
    other = shift(lax.dynamic_slice_in_dim(part, 1 - me, 1, dim).astype(BF16), "xh", 1)
    return lax.dynamic_slice_in_dim(part, me, 1, dim) + other.astype(F32)


def outer_step(current, moment, average):
    moment_new = 0.9 * moment + average
    return (current - 0.7 * (average + 0.9 * moment_new), moment_new)


def per_device(
    hidden_in,
    norm_gain,
    key_weight,
    key_cotangent,
    outer_params,
    outer_momentum,
    inner_params,
    fragment_index,
):
    hidden = hidden_in[0]
    gain_row = norm_gain[0]
    cotangent = key_cotangent[0]
    own = key_weight[0]
    rows, width = own.shape
    cut = width // 2
    groups = SIZE["xh"], SIZE["y"], SIZE["z"]
    devices = groups[0] * groups[1] * groups[2]
    factor = float(hidden.shape[0] * devices) ** (-0.5)

    pair = jnp.zeros((2, 1, 1, rows, width), BF16)
    pair = place(pair, own[None, None, None], "xh", 0, 0)
    pair = place(pair, shift(own, "xh", 1)[None, None, None], "xh", 0, 1)
    a_part, b_part = pair[..., :cut], pair[..., cut:]
    a_y = gather(jnp.zeros((2, groups[1], 1, rows, cut), BF16), a_part, "y", 1, 3)
    b_z = gather(jnp.zeros((2, 1, groups[2], rows, cut), BF16), b_part, "z", 2, 3)
    a_full = gather(jnp.zeros((*groups, rows, cut), BF16), a_y, "z", 2, 3)
    b_full = gather(jnp.zeros((*groups, rows, cut), BF16), b_z, "y", 1, 3)
    weight = jnp.concatenate([a_full, b_full], axis=-1).reshape(-1, width)

    widened = hidden.astype(F32)
    inverse = lax.rsqrt(jnp.mean(widened * widened, axis=-1, keepdims=True) + 1e-05)
    normed = widened * inverse
    scaled = (normed * gain_row[None, :]).astype(BF16)

    def summed_columns(cols, first, second):
        part = lax.dot_general(
            scaled, cols, (((0,), (0,)), ((), ())), preferred_element_type=F32
        ).reshape(*groups, rows, cut)
        for axis in (first, second):
            part = scatter_sum(part, axis, 1 if axis == "y" else 2, 3)
        return swap_sum(part, 0).reshape(rows, cut)

    grad_a = summed_columns(cotangent[:, :cut], "z", "y")
    grad_b = summed_columns(cotangent[:, cut:], "y", "z")
    grad_weight = jnp.concatenate([grad_a, grad_b], axis=-1) * factor

    me = lax.axis_index(GROUP)
    own_gain = lax.dynamic_slice_in_dim(gain_row, me * rows, rows)
    own_sum = jnp.sum(own.astype(F32) * grad_weight, axis=-1) / own_gain
    grad_gain = lax.all_to_all(
        jnp.broadcast_to(own_sum[None], (devices, rows)), GROUP, 0, 0, tiled=True
    ).reshape(-1)

    key_out = jnp.dot(scaled, weight, preferred_element_type=F32).astype(BF16)
    grad_normed = lax.dot_general(
        cotangent, weight, (((1,), (1,)), ((), ())), preferred_element_type=F32
    )
    weighted = grad_normed * gain_row[None, :]
    inner_mean = jnp.mean(weighted * normed, axis=-1, keepdims=True)
    grad_hidden = (inverse * (weighted - normed * inner_mean)).astype(BF16)

    chosen = fragment_index[0]
    current = lax.dynamic_index_in_dim(outer_params, chosen, 0, keepdims=False)
    moment = lax.dynamic_index_in_dim(outer_momentum, chosen, 0, keepdims=False)
    inner_now = lax.dynamic_index_in_dim(inner_params[0], chosen, 0, keepdims=False)
    summed = lax.psum(current - inner_now, REPL)
    new_params, new_momentum = outer_step(current, moment, summed / 4.0)
    return (
        key_out[None],
        grad_weight[None],
        grad_hidden[None],
        grad_gain[None],
        new_params,
        new_momentum,
    )


def solution(mesh):
    fine = Mesh(mesh.devices.reshape(2, 2, 2, 4, 8), (*REPL, *GROUP))
    placed = (
        P(REPL, GROUP, None),
        P(REPL, None),
        P(REPL, GROUP, None),
        P(REPL, GROUP, None),
        P(None, GROUP, None),
        P(None, GROUP, None),
        P(REPL, None, GROUP, None),
        P(),
    )
    return jax.shard_map(
        per_device,
        mesh=fine,
        in_specs=placed,
        out_specs=(
            P(REPL, GROUP, None),
            P(REPL, GROUP, None),
            P(REPL, GROUP, None),
            P(REPL, None),
            P(GROUP, None),
            P(GROUP, None),
        ),
        check_vma=False,
    )
```

```python
import functools

import jax
import jax.numpy as jnp
from jax import lax
from jax.experimental import pallas as pl
from jax.experimental.pallas import tpu as pltpu
from jax.sharding import Mesh
from jax.sharding import PartitionSpec as P

GROUP = ("xh", "y", "z")
REPL = ("xl", "core")
SIZE = {"xh": 2, "y": 4, "z": 8}
BF16 = jnp.bfloat16
F32 = jnp.float32
LANES = 128


def shift(value, axis, step):
    n = SIZE[axis]
    return lax.ppermute(value, axis, [(i, (i + step) % n) for i in range(n)])


def gather(own, axis):
    n = SIZE[axis]
    blocks = {0: own}
    right = left = own
    for hop in range(1, n // 2 + 1):
        right = shift(right, axis, 1)
        blocks[hop] = right
        if hop < n - hop:
            left = shift(left, axis, -1)
            blocks[n - hop] = left
    return [blocks[i] for i in range(n)]


def scatter_sum(part, axis, dim):
    n = SIZE[axis]

    def term(step):
        at = (lax.axis_index(axis) + step) & (n - 1)
        return lax.dynamic_slice_in_dim(part, at, 1, dim)

    left = shift(term(-(n // 2)).astype(BF16), axis, -1)
    right = None
    for hop in range(n // 2 - 1, 0, -1):
        ahead, behind = term(hop), term(-hop) + left.astype(F32)
        if right is not None:
            ahead = ahead + right.astype(F32)
        right = shift(ahead.astype(BF16), axis, 1)
        left = shift(behind.astype(BF16), axis, -1)
    return term(0) + right.astype(F32) + left.astype(F32)


def swap_sum(part, dim):
    me = lax.axis_index("xh")
    other = shift(lax.dynamic_slice_in_dim(part, 1 - me, 1, dim).astype(BF16), "xh", 1)
    return lax.dynamic_slice_in_dim(part, me, 1, dim) + other.astype(F32)


def weight_grad_kernel(hidden, gain, cotangent, a_out, b_out, inv_out, inverse, turned):
    step = pl.program_id(0)
    tokens, width = hidden.shape
    blocks, cut, _ = a_out.shape
    span = blocks * LANES

    @pl.when(step == 0)
    def _():
        def add(i, total):
            piece = hidden[:, pl.ds(pl.multiple_of(i * 512, 512), 512)].astype(F32)
            square = piece * piece
            for j in range(4):
                total = total + square[:, j * LANES : (j + 1) * LANES]
            return total

        total = lax.fori_loop(0, width // 512, add, jnp.zeros((tokens, LANES), F32))
        mean = jnp.sum(total, axis=-1, keepdims=True) / width
        inverse[...] = jnp.broadcast_to(lax.rsqrt(mean + 1e-05), (tokens, LANES))
        inv_out[...] = inverse[...]
        turned[...] = cotangent[...].T

    for j in range(0, blocks, 2):
        at = pl.ds(pl.multiple_of(step * span + j * LANES, 2 * LANES), 2 * LANES)
        scaled = (hidden[:, at].astype(F32) * inverse[:, :1] * gain[:, at]).astype(BF16)
        both = jnp.dot(turned[...], scaled, preferred_element_type=F32)
        for i in range(2):
            lanes = slice(i * LANES, (i + 1) * LANES)
            a_out[j + i] = both[:cut, lanes]
            b_out[j + i] = both[cut:, lanes]


def weight_grad(hidden, gain, cotangent):
    tokens, width = hidden.shape
    keys = cotangent.shape[1]
    blocks, per_step, cut = width // LANES, 8, keys // 2
    whole = lambda i: (0, 0)
    part = jax.ShapeDtypeStruct((blocks, cut, LANES), F32)
    return pl.pallas_call(
        weight_grad_kernel,
        grid=(blocks // per_step,),
        out_shape=(part, part, jax.ShapeDtypeStruct((tokens, LANES), F32)),
        in_specs=[
            pl.BlockSpec((tokens, width), whole),
            pl.BlockSpec((1, width), whole),
            pl.BlockSpec((tokens, keys), whole),
        ],
        out_specs=(
            pl.BlockSpec((per_step, cut, LANES), lambda i: (i, 0, 0)),
            pl.BlockSpec((per_step, cut, LANES), lambda i: (i, 0, 0)),
            pl.BlockSpec((tokens, LANES), whole),
        ),
        scratch_shapes=[pltpu.VMEM((tokens, LANES), F32), pltpu.VMEM((keys, tokens), BF16)],
        compiler_params=pltpu.CompilerParams(vmem_limit_bytes=32 * 1024 * 1024),
        cost_estimate=pl.CostEstimate(
            flops=2 * tokens * width * keys, bytes_accessed=22 * 1024 * 1024, transcendentals=0
        ),
        name="weight_grad",
    )(hidden, gain, cotangent)


def tail_kernel(na, nb, place, hidden, gain, cotangent, inverse, *refs):
    a_hbm, b_hbm = refs[:na], refs[na : na + nb]
    key_out, grad_hidden, a_all, b_all, grad, key_a, key_b, dots, sems = refs[na + nb :]
    tokens, width = hidden.shape
    cut = key_a.shape[1]
    x, y, z = place[0], place[1], place[2]
    copies = [pltpu.make_async_copy(ref, a_all.at[i], sems.at[i]) for i, ref in enumerate(a_hbm)]
    copies += [
        pltpu.make_async_copy(ref, b_all.at[i], sems.at[na + i]) for i, ref in enumerate(b_hbm)
    ]
    for copy in copies:
        copy.start()
    key_a[...] = jnp.zeros_like(key_a)
    key_b[...] = jnp.zeros_like(key_b)
    dots[...] = jnp.zeros_like(dots)

    def lanes_of(xr, yr, zr):
        block = (x ^ xr) * 32 + ((y - yr) & 3) * 8 + ((z - zr) & 7)
        return pl.ds(pl.multiple_of(block * LANES, LANES), LANES)

    def normed_at(at):
        return hidden[:, at].astype(F32) * inverse[...]

    for copy in copies[:na]:
        copy.wait()

    def a_step(zr, carry):
        rows = a_all[zr]
        grads = lax.dot_general(
            cotangent[:, :cut], rows, (((1,), (1,)), ((), ())), preferred_element_type=F32
        )
        scaled = []
        for i in range(8):
            at = lanes_of(i % 2, i // 2, zr)
            grad[:, at] = grads[:, i * LANES : (i + 1) * LANES]
            scaled.append((normed_at(at) * gain[:, at]).astype(BF16))
        key_a[...] += jnp.dot(
            jnp.concatenate(scaled, axis=1), rows, preferred_element_type=F32
        )
        return carry

    lax.fori_loop(0, na, a_step, 0)
    for copy in copies[na:]:
        copy.wait()

    def b_step(i, carry):
        yr, half = i // 2, i % 2
        rows = b_all[yr, pl.ds(pl.multiple_of(half * 1024, 1024), 1024), :]
        grads = lax.dot_general(
            cotangent[:, cut:], rows, (((1,), (1,)), ((), ())), preferred_element_type=F32
        )
        scaled = []
        total = dots[...]
        for j in range(8):
            at = lanes_of(j % 2, yr, half * 4 + j // 2)
            full = grad[:, at] + grads[:, j * LANES : (j + 1) * LANES]
            weighted = full * gain[:, at]
            normed = normed_at(at)
            grad[:, at] = weighted
            total = total + weighted * normed
            scaled.append((normed * gain[:, at]).astype(BF16))
        dots[...] = total
        key_b[...] += jnp.dot(
            jnp.concatenate(scaled, axis=1), rows, preferred_element_type=F32
        )
        return carry

    lax.fori_loop(0, 2 * nb, b_step, 0)
    key_out[:, :cut] = key_a[...].astype(BF16)
    key_out[:, cut:] = key_b[...].astype(BF16)
    mean = jnp.sum(dots[...], axis=-1, keepdims=True) / width

    def finish(i, carry):
        at = pl.ds(pl.multiple_of(i * 512, 512), 512)
        inv = inverse[:, :1]
        normed = hidden[:, at].astype(F32) * inv
        grad_hidden[:, at] = (inv * (grad[:, at] - normed * mean)).astype(BF16)
        return carry

    lax.fori_loop(0, width // 512, finish, 0)


def tail(place, hidden, gain, cotangent, inverse, a_blocks, b_blocks):
    tokens, width = hidden.shape
    keys = cotangent.shape[1]
    cut = keys // 2
    na, nb = len(a_blocks), len(b_blocks)
    vmem = pl.BlockSpec(memory_space=pltpu.VMEM)
    return pl.pallas_call(
        functools.partial(tail_kernel, na, nb),
        out_shape=(
            jax.ShapeDtypeStruct((tokens, keys), BF16),
            jax.ShapeDtypeStruct((tokens, width), BF16),
        ),
        in_specs=[pl.BlockSpec(memory_space=pltpu.SMEM)]
        + [vmem] * 4
        + [pl.BlockSpec(memory_space=pl.ANY)] * (na + nb),
        out_specs=(vmem, vmem),
        scratch_shapes=[
            pltpu.VMEM((na, width // na, cut), BF16),
            pltpu.VMEM((nb, width // nb, cut), BF16),
            pltpu.VMEM((tokens, width), F32),
            pltpu.VMEM((tokens, cut), F32),
            pltpu.VMEM((tokens, cut), F32),
            pltpu.VMEM((tokens, LANES), F32),
            pltpu.SemaphoreType.DMA((na + nb,)),
        ],
        compiler_params=pltpu.CompilerParams(vmem_limit_bytes=40 * 1024 * 1024),
        cost_estimate=pl.CostEstimate(
            flops=4 * tokens * width * keys, bytes_accessed=18 * 1024 * 1024, transcendentals=0
        ),
        name="tail",
    )(place, hidden, gain, cotangent, inverse, *a_blocks, *b_blocks)


def outer_step(current, moment, average):
    moment_new = 0.9 * moment + average
    return (current - 0.7 * (average + 0.9 * moment_new), moment_new)


def per_device(
    hidden_in,
    norm_gain,
    key_weight,
    key_cotangent,
    outer_params,
    outer_momentum,
    inner_params,
    fragment_index,
):
    hidden = hidden_in[0]
    cotangent = key_cotangent[0]
    own = key_weight[0]
    rows, width = own.shape
    cut = width // 2
    groups = SIZE["xh"], SIZE["y"], SIZE["z"]
    devices = groups[0] * groups[1] * groups[2]
    factor = float(hidden.shape[0] * devices) ** (-0.5)

    chosen = fragment_index[0]
    current = lax.dynamic_index_in_dim(outer_params, chosen, 0, keepdims=False)
    inner_now = lax.dynamic_index_in_dim(inner_params[0], chosen, 0, keepdims=False)
    summed = lax.psum(current - inner_now, REPL)

    other = shift(own, "xh", 1)
    part_a, part_b, inverse = weight_grad(hidden, norm_gain, cotangent)
    other, inverse = lax.optimization_barrier((other, inverse))

    def summed_columns(part, first, second):
        part = part.reshape(*groups, cut, rows)
        for axis in (first, second):
            part = scatter_sum(part, axis, 1 if axis == "y" else 2)
        return swap_sum(part, 0).reshape(cut, rows)

    grad_a = summed_columns(part_a, "z", "y")
    grad_b = summed_columns(part_b, "y", "z")
    grad_weight = jnp.concatenate([grad_a.T, grad_b.T], axis=-1) * factor

    pair = jnp.concatenate([own, other])
    a_blocks = gather(jnp.concatenate(gather(pair[:, :cut], "y")), "z")
    b_blocks = gather(jnp.concatenate(gather(pair[:, cut:], "z")), "y")

    me = lax.axis_index(GROUP)
    own_gain = lax.dynamic_slice_in_dim(norm_gain[0], me * rows, rows)
    own_sum = jnp.sum(own.astype(F32) * grad_weight, axis=-1) / own_gain
    grad_gain = lax.all_to_all(
        jnp.broadcast_to(own_sum[None], (devices, rows)), GROUP, 0, 0, tiled=True
    ).reshape(-1)

    place = jnp.stack([lax.axis_index(axis) for axis in GROUP])
    key_out, grad_hidden = tail(
        place, hidden, norm_gain, cotangent, inverse, a_blocks, b_blocks
    )

    summed, grad_gain = lax.optimization_barrier((summed, grad_gain))
    moment = lax.dynamic_index_in_dim(outer_momentum, chosen, 0, keepdims=False)
    new_params, new_momentum = outer_step(current, moment, summed / 4.0)
    return (
        key_out[None],
        grad_weight[None],
        grad_hidden[None],
        grad_gain[None],
        new_params,
        new_momentum,
    )


def solution(mesh):
    fine = Mesh(mesh.devices.reshape(2, 2, 2, 4, 8), (*REPL, *GROUP))
    placed = (
        P(REPL, GROUP, None),
        P(REPL, None),
        P(REPL, GROUP, None),
        P(REPL, GROUP, None),
        P(None, GROUP, None),
        P(None, GROUP, None),
        P(REPL, None, GROUP, None),
        P(),
    )
    return jax.shard_map(
        per_device,
        mesh=fine,
        in_specs=placed,
        out_specs=(
            P(REPL, GROUP, None),
            P(REPL, GROUP, None),
            P(REPL, GROUP, None),
            P(REPL, None),
            P(GROUP, None),
            P(GROUP, None),
        ),
        check_vma=False,
    )
```

```python
import functools

import jax
import jax.numpy as jnp
from jax import lax
from jax.experimental import pallas as pl
from jax.experimental.pallas import tpu as pltpu
from jax.sharding import Mesh
from jax.sharding import PartitionSpec as P

GROUP = ("xh", "y", "z")
REPL = ("xl", "core")
SIZE = {"xh": 2, "y": 4, "z": 8}
BF16 = jnp.bfloat16
F32 = jnp.float32
LANES = 128
FIRST = (0, 1, 7, 2)
SECOND = (6, 3, 5, 4)


def shift(value, axis, step):
    n = SIZE[axis]
    return lax.ppermute(value, axis, [(i, (i + step) % n) for i in range(n)])


def gather(own, axis, last):
    n = SIZE[axis]
    blocks = {0: own}
    right = left = own
    for hop in range(1, n // 2):
        right, left = shift(right, axis, 1), shift(left, axis, -1)
        blocks[hop], blocks[n - hop] = right, left
    blocks[n // 2] = shift(right if last > 0 else left, axis, last)
    return [blocks[i] for i in range(n)]


def scatter_sum(part, axis, dim):
    n = SIZE[axis]

    def term(step):
        at = (lax.axis_index(axis) + step) & (n - 1)
        return lax.dynamic_slice_in_dim(part, at, 1, dim)

    left = shift(term(-(n // 2)).astype(BF16), axis, -1)
    right = None
    for hop in range(n // 2 - 1, 0, -1):
        ahead, behind = term(hop), term(-hop) + left.astype(F32)
        if right is not None:
            ahead = ahead + right.astype(F32)
        right = shift(ahead.astype(BF16), axis, 1)
        left = shift(behind.astype(BF16), axis, -1)
    return term(0) + right.astype(F32) + left.astype(F32)


def exchange_sum(part, axes):
    blocks = lax.all_to_all(part.astype(BF16), axes, 0, 0, tiled=True)
    return jnp.sum(blocks.astype(F32), axis=0)


def weight_grad_kernel(hidden, gain, cotangent, a_out, b_out, inv_out, inverse, turned):
    step = pl.program_id(0)
    tokens, width = hidden.shape
    blocks, cut, _ = a_out.shape
    span = blocks * LANES

    @pl.when(step == 0)
    def _():
        def add(i, total):
            piece = hidden[:, pl.ds(pl.multiple_of(i * 512, 512), 512)].astype(F32)
            square = piece * piece
            for j in range(4):
                total = total + square[:, j * LANES : (j + 1) * LANES]
            return total

        total = lax.fori_loop(0, width // 512, add, jnp.zeros((tokens, LANES), F32))
        mean = jnp.sum(total, axis=-1, keepdims=True) / width
        inverse[...] = jnp.broadcast_to(lax.rsqrt(mean + 1e-05), (tokens, LANES))
        inv_out[...] = inverse[...]
        turned[...] = cotangent[...].T

    for j in range(0, blocks, 2):
        at = pl.ds(pl.multiple_of(step * span + j * LANES, 2 * LANES), 2 * LANES)
        scaled = (hidden[:, at].astype(F32) * inverse[:, :1] * gain[:, at]).astype(BF16)
        both = jnp.dot(turned[...], scaled, preferred_element_type=F32)
        for i in range(2):
            lanes = slice(i * LANES, (i + 1) * LANES)
            a_out[j + i] = both[:cut, lanes]
            b_out[j + i] = both[cut:, lanes]


def weight_grad(hidden, gain, cotangent):
    tokens, width = hidden.shape
    keys = cotangent.shape[1]
    blocks, per_step, cut = width // LANES, 8, keys // 2
    whole = lambda i: (0, 0)
    part = jax.ShapeDtypeStruct((blocks, cut, LANES), F32)
    return pl.pallas_call(
        weight_grad_kernel,
        grid=(blocks // per_step,),
        out_shape=(part, part, jax.ShapeDtypeStruct((tokens, LANES), F32)),
        in_specs=[
            pl.BlockSpec((tokens, width), whole),
            pl.BlockSpec((1, width), whole),
            pl.BlockSpec((tokens, keys), whole),
        ],
        out_specs=(
            pl.BlockSpec((per_step, cut, LANES), lambda i: (i, 0, 0)),
            pl.BlockSpec((per_step, cut, LANES), lambda i: (i, 0, 0)),
            pl.BlockSpec((tokens, LANES), whole),
        ),
        scratch_shapes=[pltpu.VMEM((tokens, LANES), F32), pltpu.VMEM((keys, tokens), BF16)],
        compiler_params=pltpu.CompilerParams(vmem_limit_bytes=32 * 1024 * 1024),
        cost_estimate=pl.CostEstimate(
            flops=2 * tokens * width * keys, bytes_accessed=22 * 1024 * 1024, transcendentals=0
        ),
        name="weight_grad",
    )(hidden, gain, cotangent)


def tail_kernel(count, place, hidden, gain, cotangent, inverse, *refs):
    weights = refs[:count]
    key_out, grad_hidden, held, grad, keys, dots, sems = refs[count:]
    tokens, width = hidden.shape
    x, y, z = place[0], place[1], place[2]
    for i, ref in enumerate(weights):
        pltpu.make_async_copy(ref, held.at[i], sems.at[i]).start()
    keys[...] = jnp.zeros_like(keys)
    dots[...] = jnp.zeros_like(dots)

    def block(i, carry):
        pltpu.make_async_copy(held.at[i], held.at[i], sems.at[i]).wait()
        rows = held[i]
        grads = lax.dot_general(
            cotangent[...], rows, (((1,), (1,)), ((), ())), preferred_element_type=F32
        )
        scaled = []
        total = dots[...]
        for j in range(8):
            zr = jnp.where(i % 2 == 0, FIRST[j // 2], SECOND[j // 2])
            feature = (x ^ (j % 2)) * 32 + ((y - i // 2) & 3) * 8 + ((z - zr) & 7)
            at = pl.ds(pl.multiple_of(feature * LANES, LANES), LANES)
            normed = hidden[:, at].astype(F32) * inverse[...]
            weighted = grads[:, j * LANES : (j + 1) * LANES] * gain[:, at]
            grad[:, at] = weighted
            total = total + weighted * normed
            scaled.append((normed * gain[:, at]).astype(BF16))
        dots[...] = total
        keys[...] += jnp.dot(
            jnp.concatenate(scaled, axis=1), rows, preferred_element_type=F32
        )
        return carry

    lax.fori_loop(0, count, block, 0)
    key_out[...] = keys[...].astype(BF16)
    mean = jnp.sum(dots[...], axis=-1, keepdims=True) / width

    def finish(i, carry):
        at = pl.ds(pl.multiple_of(i * 512, 512), 512)
        inv = inverse[:, :1]
        normed = hidden[:, at].astype(F32) * inv
        grad_hidden[:, at] = (inv * (grad[:, at] - normed * mean)).astype(BF16)
        return carry

    lax.fori_loop(0, width // 512, finish, 0)


def tail(place, hidden, gain, cotangent, inverse, weights):
    tokens, width = hidden.shape
    keys = cotangent.shape[1]
    count = len(weights)
    vmem = pl.BlockSpec(memory_space=pltpu.VMEM)
    return pl.pallas_call(
        functools.partial(tail_kernel, count),
        out_shape=(
            jax.ShapeDtypeStruct((tokens, keys), BF16),
            jax.ShapeDtypeStruct((tokens, width), BF16),
        ),
        in_specs=[pl.BlockSpec(memory_space=pltpu.SMEM)]
        + [vmem] * 4
        + [pl.BlockSpec(memory_space=pl.ANY)] * count,
        out_specs=(vmem, vmem),
        scratch_shapes=[
            pltpu.VMEM((count, width // count, keys), BF16),
            pltpu.VMEM((tokens, width), F32),
            pltpu.VMEM((tokens, keys), F32),
            pltpu.VMEM((tokens, LANES), F32),
            pltpu.SemaphoreType.DMA((count,)),
        ],
        compiler_params=pltpu.CompilerParams(vmem_limit_bytes=40 * 1024 * 1024),
        cost_estimate=pl.CostEstimate(
            flops=4 * tokens * width * keys, bytes_accessed=18 * 1024 * 1024, transcendentals=0
        ),
        name="tail",
    )(place, hidden, gain, cotangent, inverse, *weights)


def outer_step(current, moment, average):
    moment_new = 0.9 * moment + average
    return (current - 0.7 * (average + 0.9 * moment_new), moment_new)


def per_device(
    hidden_in,
    norm_gain,
    key_weight,
    key_cotangent,
    outer_params,
    outer_momentum,
    inner_params,
    fragment_index,
):
    hidden = hidden_in[0]
    cotangent = key_cotangent[0]
    own = key_weight[0]
    rows, width = own.shape
    cut = width // 2
    groups = SIZE["xh"], SIZE["y"], SIZE["z"]
    devices = groups[0] * groups[1] * groups[2]
    factor = float(hidden.shape[0] * devices) ** (-0.5)

    chosen = fragment_index[0]
    current = lax.dynamic_index_in_dim(outer_params, chosen, 0, keepdims=False)
    inner_now = lax.dynamic_index_in_dim(inner_params[0], chosen, 0, keepdims=False)
    summed = current - inner_now
    for axis in REPL:
        summed = summed + lax.ppermute(summed, axis, [(0, 1), (1, 0)])

    pair = jnp.concatenate([own, shift(own, "xh", 1)])
    along_z = gather(pair, "z", 1)
    first = gather(jnp.concatenate([along_z[i] for i in FIRST]), "y", 1)
    second = gather(jnp.concatenate([along_z[i] for i in SECOND]), "y", -1)
    weights = [block for both in zip(first, second) for block in both]

    part_a, part_b, inverse = weight_grad(hidden, norm_gain, cotangent)
    part_a = part_a.reshape(*groups, cut, rows)
    part_b = part_b.reshape(*groups, cut, rows)
    sum_a = exchange_sum(scatter_sum(part_a, "z", 2).reshape(-1, cut, rows), ("xh", "y"))
    sum_b = exchange_sum(scatter_sum(part_b, "y", 1).reshape(-1, cut, rows), ("xh", "z"))
    sum_a, sum_b = lax.optimization_barrier((sum_a, sum_b))
    grad_weight = jnp.concatenate([sum_a.T, sum_b.T], axis=-1) * factor

    me = lax.axis_index(GROUP)
    own_gain = lax.dynamic_slice_in_dim(norm_gain[0], me * rows, rows)
    own_sum = jnp.sum(own.astype(F32) * grad_weight, axis=-1) / own_gain
    grad_gain = lax.all_to_all(
        jnp.broadcast_to(own_sum[None], (devices, rows)), GROUP, 0, 0, tiled=True
    ).reshape(-1)

    place = jnp.stack([lax.axis_index(axis) for axis in GROUP])
    key_out, grad_hidden = tail(place, hidden, norm_gain, cotangent, inverse, weights)

    moment = lax.dynamic_index_in_dim(outer_momentum, chosen, 0, keepdims=False)
    new_params, new_momentum = outer_step(current, moment, summed / 4.0)
    return (
        key_out[None],
        grad_weight[None],
        grad_hidden[None],
        grad_gain[None],
        new_params,
        new_momentum,
    )


def solution(mesh):
    fine = Mesh(mesh.devices.reshape(2, 2, 2, 4, 8), (*REPL, *GROUP))
    placed = (
        P(REPL, GROUP, None),
        P(REPL, None),
        P(REPL, GROUP, None),
        P(REPL, GROUP, None),
        P(None, GROUP, None),
        P(None, GROUP, None),
        P(REPL, None, GROUP, None),
        P(),
    )
    return jax.shard_map(
        per_device,
        mesh=fine,
        in_specs=placed,
        out_specs=(
            P(REPL, GROUP, None),
            P(REPL, GROUP, None),
            P(REPL, GROUP, None),
            P(REPL, None),
            P(GROUP, None),
            P(GROUP, None),
        ),
        check_vma=False,
    )
```

```python
import functools

import jax
import jax.numpy as jnp
from jax import lax
from jax.experimental import pallas as pl
from jax.experimental.pallas import tpu as pltpu
from jax.sharding import Mesh
from jax.sharding import PartitionSpec as P

GROUP = ("xh", "y", "z")
REPL = ("xl", "core")
SIZE = {"xh": 2, "y": 4, "z": 8}
BF16 = jnp.bfloat16
F32 = jnp.float32
LANES = 128
FIRST = (0, 1, 7, 2)
SECOND = (6, 3, 5, 4)


def shift(value, axis, step):
    n = SIZE[axis]
    return lax.ppermute(value, axis, [(i, (i + step) % n) for i in range(n)])


def together(*values):
    return lax.optimization_barrier(values)


def term(part, axis, dim, step):
    at = (lax.axis_index(axis) + step) & (SIZE[axis] - 1)
    return lax.dynamic_slice_in_dim(part, at, 1, dim)


def onward(part, axis, dim, step, received):
    total = term(part, axis, dim, step) + received.astype(F32)
    return shift(total.astype(BF16), axis, 1 if step > 0 else -1)


def exchange_sum(part, axes):
    blocks = lax.all_to_all(part.astype(BF16), axes, 0, 0, tiled=True)
    return jnp.sum(blocks.astype(F32), axis=0)


def weight_grad_kernel(hidden, gain, cotangent, a_out, b_out, inv_out, inverse, turned):
    step = pl.program_id(0)
    tokens, width = hidden.shape
    blocks, cut, _ = a_out.shape
    span = blocks * LANES

    @pl.when(step == 0)
    def _():
        def add(i, total):
            piece = hidden[:, pl.ds(pl.multiple_of(i * 512, 512), 512)].astype(F32)
            square = piece * piece
            for j in range(4):
                total = total + square[:, j * LANES : (j + 1) * LANES]
            return total

        total = lax.fori_loop(0, width // 512, add, jnp.zeros((tokens, LANES), F32))
        mean = jnp.sum(total, axis=-1, keepdims=True) / width
        inverse[...] = jnp.broadcast_to(lax.rsqrt(mean + 1e-05), (tokens, LANES))
        inv_out[...] = inverse[...]
        turned[...] = cotangent[...].T

    for j in range(0, blocks, 2):
        at = pl.ds(pl.multiple_of(step * span + j * LANES, 2 * LANES), 2 * LANES)
        scaled = (hidden[:, at].astype(F32) * inverse[:, :1] * gain[:, at]).astype(BF16)
        both = jnp.dot(turned[...], scaled, preferred_element_type=F32)
        for i in range(2):
            lanes = slice(i * LANES, (i + 1) * LANES)
            a_out[j + i] = both[:cut, lanes]
            b_out[j + i] = both[cut:, lanes]


def weight_grad(hidden, gain, cotangent):
    tokens, width = hidden.shape
    keys = cotangent.shape[1]
    blocks, per_step, cut = width // LANES, 8, keys // 2
    whole = lambda i: (0, 0)
    part = jax.ShapeDtypeStruct((blocks, cut, LANES), F32)
    return pl.pallas_call(
        weight_grad_kernel,
        grid=(blocks // per_step,),
        out_shape=(part, part, jax.ShapeDtypeStruct((tokens, LANES), F32)),
        in_specs=[
            pl.BlockSpec((tokens, width), whole),
            pl.BlockSpec((1, width), whole),
            pl.BlockSpec((tokens, keys), whole),
        ],
        out_specs=(
            pl.BlockSpec((per_step, cut, LANES), lambda i: (i, 0, 0)),
            pl.BlockSpec((per_step, cut, LANES), lambda i: (i, 0, 0)),
            pl.BlockSpec((tokens, LANES), whole),
        ),
        scratch_shapes=[pltpu.VMEM((tokens, LANES), F32), pltpu.VMEM((keys, tokens), BF16)],
        compiler_params=pltpu.CompilerParams(vmem_limit_bytes=56 * 1024 * 1024),
        cost_estimate=pl.CostEstimate(
            flops=2 * tokens * width * keys, bytes_accessed=22 * 1024 * 1024, transcendentals=0
        ),
        name="weight_grad",
    )(hidden, gain, cotangent)


def tail_kernel(count, place, hidden, gain, cotangent, inverse, *refs):
    weights = refs[:count]
    key_out, grad_hidden, held, grad, keys, dots, sems = refs[count:]
    tokens, width = hidden.shape
    x, y, z = place[0], place[1], place[2]
    for i, ref in enumerate(weights):
        pltpu.make_async_copy(ref, held.at[i], sems.at[i]).start()
    keys[...] = jnp.zeros_like(keys)
    dots[...] = jnp.zeros_like(dots)

    def block(i, carry):
        pltpu.make_async_copy(held.at[i], held.at[i], sems.at[i]).wait()
        rows = held[i]
        grads = lax.dot_general(
            cotangent[...], rows, (((1,), (1,)), ((), ())), preferred_element_type=F32
        )
        scaled = []
        total = dots[...]
        for j in range(8):
            zr = jnp.where(i % 2 == 0, FIRST[j // 2], SECOND[j // 2])
            feature = (x ^ (j % 2)) * 32 + ((y - i // 2) & 3) * 8 + ((z - zr) & 7)
            at = pl.ds(pl.multiple_of(feature * LANES, LANES), LANES)
            normed = hidden[:, at].astype(F32) * inverse[...]
            weighted = grads[:, j * LANES : (j + 1) * LANES] * gain[:, at]
            grad[:, at] = weighted
            total = total + weighted * normed
            scaled.append((normed * gain[:, at]).astype(BF16))
        dots[...] = total
        keys[...] += jnp.dot(
            jnp.concatenate(scaled, axis=1), rows, preferred_element_type=F32
        )
        return carry

    lax.fori_loop(0, count, block, 0)
    key_out[...] = keys[...].astype(BF16)
    mean = jnp.sum(dots[...], axis=-1, keepdims=True) / width

    def finish(i, carry):
        at = pl.ds(pl.multiple_of(i * 512, 512), 512)
        inv = inverse[:, :1]
        normed = hidden[:, at].astype(F32) * inv
        grad_hidden[:, at] = (inv * (grad[:, at] - normed * mean)).astype(BF16)
        return carry

    lax.fori_loop(0, width // 512, finish, 0)


def tail(place, hidden, gain, cotangent, inverse, weights):
    tokens, width = hidden.shape
    keys = cotangent.shape[1]
    count = len(weights)
    vmem = pl.BlockSpec(memory_space=pltpu.VMEM)
    return pl.pallas_call(
        functools.partial(tail_kernel, count),
        out_shape=(
            jax.ShapeDtypeStruct((tokens, keys), BF16),
            jax.ShapeDtypeStruct((tokens, width), BF16),
        ),
        in_specs=[pl.BlockSpec(memory_space=pltpu.SMEM)]
        + [vmem] * 4
        + [pl.BlockSpec(memory_space=pl.ANY)] * count,
        out_specs=(vmem, vmem),
        scratch_shapes=[
            pltpu.VMEM((count, width // count, keys), BF16),
            pltpu.VMEM((tokens, width), F32),
            pltpu.VMEM((tokens, keys), F32),
            pltpu.VMEM((tokens, LANES), F32),
            pltpu.SemaphoreType.DMA((count,)),
        ],
        compiler_params=pltpu.CompilerParams(vmem_limit_bytes=40 * 1024 * 1024),
        cost_estimate=pl.CostEstimate(
            flops=4 * tokens * width * keys, bytes_accessed=18 * 1024 * 1024, transcendentals=0
        ),
        name="tail",
    )(place, hidden, gain, cotangent, inverse, *weights)


def outer_step(current, moment, average):
    moment_new = 0.9 * moment + average
    return (current - 0.7 * (average + 0.9 * moment_new), moment_new)


def per_device(
    hidden_in,
    norm_gain,
    key_weight,
    key_cotangent,
    outer_params,
    outer_momentum,
    inner_params,
    fragment_index,
):
    hidden = hidden_in[0]
    cotangent = key_cotangent[0]
    own = key_weight[0]
    rows, width = own.shape
    cut = width // 2
    groups = SIZE["xh"], SIZE["y"], SIZE["z"]
    devices = groups[0] * groups[1] * groups[2]
    factor = float(hidden.shape[0] * devices) ** (-0.5)

    chosen = fragment_index[0]
    current = lax.dynamic_index_in_dim(outer_params, chosen, 0, keepdims=False)
    inner_now = lax.dynamic_index_in_dim(inner_params[0], chosen, 0, keepdims=False)
    part_a, part_b, inverse = weight_grad(hidden, norm_gain, cotangent)
    part_a = part_a.reshape(*groups, cut, rows)
    part_b = part_b.reshape(*groups, cut, rows)
    half = cut // 2

    mine = current - inner_now
    over_x = shift(own, "xh", 1)
    core = lax.ppermute(mine, "core", [(0, 1), (1, 0)])
    over_x, part_a, part_b, inverse, core = together(over_x, part_a, part_b, inverse, core)
    pair = jnp.concatenate([own, over_x])

    far_a = term(part_a, "z", 2, -4).astype(BF16)
    far_b = term(part_b, "y", 1, 2).astype(BF16)
    a_left = shift(far_a, "z", -1)
    z1, z7 = shift(pair, "z", 1), shift(pair, "z", -1)
    b_left = shift(far_b[..., half:, :], "y", -1)
    b_right = shift(far_b[..., :half, :], "y", 1)
    a_left, z1, z7, b_left, b_right = together(a_left, z1, z7, b_left, b_right)

    a_left = onward(part_a, "z", 2, -3, a_left)
    a_right = shift(term(part_a, "z", 2, 3).astype(BF16), "z", 1)
    z2, z6 = shift(z1, "z", 1), shift(z7, "z", -1)
    none = jnp.zeros_like(b_left)
    b_left = onward(part_b, "y", 1, -1, jnp.concatenate([none, b_left], axis=3))
    b_right = onward(part_b, "y", 1, 1, jnp.concatenate([b_right, none], axis=3))
    a_left, a_right, z2, z6 = together(a_left, a_right, z2, z6)

    a_left = onward(part_a, "z", 2, -2, a_left)
    a_right = onward(part_a, "z", 2, 2, a_right)
    z3, z5 = shift(z2, "z", 1), shift(z6, "z", -1)
    first = jnp.concatenate([pair, z1, z7, z2])
    first1, first3 = shift(first, "y", 1), shift(first, "y", -1)
    a_left, a_right, z3, z5, b_left, b_right = together(a_left, a_right, z3, z5, b_left, b_right)

    sum_b = term(part_b, "y", 1, 0) + b_left.astype(F32) + b_right.astype(F32)
    sum_b = exchange_sum(sum_b.reshape(-1, cut, rows), ("xh", "z"))
    a_left = onward(part_a, "z", 2, -1, a_left)
    a_right = onward(part_a, "z", 2, 1, a_right)
    z4 = shift(z3, "z", 1)
    a_left, a_right, z4, first1, first3, sum_b, core = together(
        a_left, a_right, z4, first1, first3, sum_b, core
    )

    sum_a = term(part_a, "z", 2, 0) + a_left.astype(F32) + a_right.astype(F32)
    sum_a = exchange_sum(sum_a.reshape(-1, cut, rows), ("xh", "y"))
    second = jnp.concatenate([z6, z3, z5, z4])
    second1, second3 = shift(second, "y", 1), shift(second, "y", -1)
    first2 = shift(first1, "y", 1)
    both = mine + core
    summed = both + lax.ppermute(both, "xl", [(0, 1), (1, 0)])
    sum_a, second1, second3, summed = together(sum_a, second1, second3, summed)
    second2 = shift(second3, "y", -1)
    weights = [first, second, first1, second1, first2, second2, first3, second3]

    grad_weight = jnp.concatenate([sum_a.T, sum_b.T], axis=-1) * factor

    me = lax.axis_index(GROUP)
    own_gain = lax.dynamic_slice_in_dim(norm_gain[0], me * rows, rows)
    own_sum = jnp.sum(own.astype(F32) * grad_weight, axis=-1) / own_gain
    place = jnp.stack([lax.axis_index(axis) for axis in GROUP])
    own_sum, weights[-1], weights[-3] = together(own_sum, weights[-1], weights[-3])
    grad_gain = lax.all_to_all(
        jnp.broadcast_to(own_sum[None], (devices, rows)), GROUP, 0, 0, tiled=True
    ).reshape(-1)
    key_out, grad_hidden = tail(place, hidden, norm_gain, cotangent, inverse, weights)

    moment = lax.dynamic_index_in_dim(outer_momentum, chosen, 0, keepdims=False)
    new_params, new_momentum = outer_step(current, moment, summed / 4.0)
    return (
        key_out[None],
        grad_weight[None],
        grad_hidden[None],
        grad_gain[None],
        new_params,
        new_momentum,
    )


def solution(mesh):
    fine = Mesh(mesh.devices.reshape(2, 2, 2, 4, 8), (*REPL, *GROUP))
    placed = (
        P(REPL, GROUP, None),
        P(REPL, None),
        P(REPL, GROUP, None),
        P(REPL, GROUP, None),
        P(None, GROUP, None),
        P(None, GROUP, None),
        P(REPL, None, GROUP, None),
        P(),
    )
    return jax.shard_map(
        per_device,
        mesh=fine,
        in_specs=placed,
        out_specs=(
            P(REPL, GROUP, None),
            P(REPL, GROUP, None),
            P(REPL, GROUP, None),
            P(REPL, None),
            P(GROUP, None),
            P(GROUP, None),
        ),
        check_vma=False,
    )
```

```python
import functools

import jax
import jax.numpy as jnp
from jax import lax
from jax.experimental import pallas as pl
from jax.experimental.pallas import tpu as pltpu
from jax.sharding import Mesh
from jax.sharding import PartitionSpec as P

GROUP = ("xh", "y", "z")
REPL = ("xl", "core")
SIZE = {"xh": 2, "y": 4, "z": 8}
BF16 = jnp.bfloat16
F32 = jnp.float32
LANES = 128
ORDER = (0, 1, 7, 2, 6, 3, 5, 4)


def shift(value, axis, step):
    n = SIZE[axis]
    return lax.ppermute(value, axis, [(i, (i + step) % n) for i in range(n)])


def together(*values):
    return lax.optimization_barrier(values)


def term(part, axis, dim, step):
    at = (lax.axis_index(axis) + step) & (SIZE[axis] - 1)
    return lax.dynamic_slice_in_dim(part, at, 1, dim)


def added(part, axis, dim, step, received):
    mine = term(part, axis, dim, step).reshape(received.shape)
    return (mine.astype(F32) + received.astype(F32)).astype(BF16)


def exchange_sum(part, axes):
    blocks = lax.all_to_all(part.astype(BF16), axes, 0, 0, tiled=True)
    return jnp.sum(blocks.astype(F32), axis=0)


def weight_grad_kernel(hidden, gain, cotangent, a_out, b_out, inv_out, inverse, turned):
    step = pl.program_id(0)
    tokens, width = hidden.shape
    blocks, cut, _ = a_out.shape
    span = blocks * LANES

    @pl.when(step == 0)
    def _():
        def add(i, total):
            piece = hidden[:, pl.ds(pl.multiple_of(i * 512, 512), 512)].astype(F32)
            square = piece * piece
            for j in range(4):
                total = total + square[:, j * LANES : (j + 1) * LANES]
            return total

        total = lax.fori_loop(0, width // 512, add, jnp.zeros((tokens, LANES), F32))
        mean = jnp.sum(total, axis=-1, keepdims=True) / width
        inverse[...] = jnp.broadcast_to(lax.rsqrt(mean + 1e-05), (tokens, LANES))
        inv_out[...] = inverse[...]
        turned[...] = cotangent[...].T

    for j in range(0, blocks, 2):
        at = pl.ds(pl.multiple_of(step * span + j * LANES, 2 * LANES), 2 * LANES)
        scaled = (hidden[:, at].astype(F32) * inverse[:, :1] * gain[:, at]).astype(BF16)
        both = jnp.dot(turned[...], scaled, preferred_element_type=F32)
        for i in range(2):
            lanes = slice(i * LANES, (i + 1) * LANES)
            a_out[j + i] = both[:cut, lanes].astype(BF16)
            b_out[j + i] = both[cut:, lanes].astype(BF16)


def weight_grad(hidden, gain, cotangent):
    tokens, width = hidden.shape
    keys = cotangent.shape[1]
    blocks, per_step, cut = width // LANES, 8, keys // 2
    whole = lambda i: (0, 0)
    part = jax.ShapeDtypeStruct((blocks, cut, LANES), BF16)
    return pl.pallas_call(
        weight_grad_kernel,
        grid=(blocks // per_step,),
        out_shape=(part, part, jax.ShapeDtypeStruct((tokens, LANES), F32)),
        in_specs=[
            pl.BlockSpec((tokens, width), whole),
            pl.BlockSpec((1, width), whole),
            pl.BlockSpec((tokens, keys), whole),
        ],
        out_specs=(
            pl.BlockSpec((per_step, cut, LANES), lambda i: (i, 0, 0)),
            pl.BlockSpec((per_step, cut, LANES), lambda i: (i, 0, 0)),
            pl.BlockSpec((tokens, LANES), whole),
        ),
        scratch_shapes=[pltpu.VMEM((tokens, LANES), F32), pltpu.VMEM((keys, tokens), BF16)],
        compiler_params=pltpu.CompilerParams(vmem_limit_bytes=56 * 1024 * 1024),
        cost_estimate=pl.CostEstimate(
            flops=2 * tokens * width * keys, bytes_accessed=22 * 1024 * 1024, transcendentals=0
        ),
        name="weight_grad",
    )(hidden, gain, cotangent)


def tail_kernel(count, place, hidden, gain, cotangent, inverse, *refs):
    weights = refs[:count]
    key_out, grad_hidden, held, grad, keys, dots, sems = refs[count:]
    tokens, width = hidden.shape
    x, y, z = place[0], place[1], place[2]
    split = weights[0].shape[1]
    places = (pl.ds(0, split), pl.ds(split, weights[1].shape[1]))
    for i, ref in enumerate(weights):
        for group in range(ref.shape[0]):
            lanes = pl.ds(group * LANES, LANES)
            there = held.at[i // 2, places[i % 2], lanes]
            pltpu.make_async_copy(ref.at[group], there, sems.at[i // 2]).start()
    keys[...] = jnp.zeros_like(keys)
    dots[...] = jnp.zeros_like(dots)

    def block(i, carry):
        yr, half = i // 2, i % 2

        @pl.when(half == 0)
        def _():
            pltpu.make_async_copy(held.at[yr], held.at[yr], sems.at[yr]).wait()

        rows = held[yr, pl.ds(pl.multiple_of(half * 1024, 1024), 1024), :]
        grads = lax.dot_general(
            cotangent[...], rows, (((1,), (1,)), ((), ())), preferred_element_type=F32
        )
        scaled = []
        total = dots[...]
        for j in range(8):
            zr = jnp.where(half == 0, ORDER[j // 2], ORDER[4 + j // 2])
            feature = (x ^ (j % 2)) * 32 + ((y - yr) & 3) * 8 + ((z - zr) & 7)
            at = pl.ds(pl.multiple_of(feature * LANES, LANES), LANES)
            normed = hidden[:, at].astype(F32) * inverse[...]
            weighted = grads[:, j * LANES : (j + 1) * LANES] * gain[:, at]
            grad[:, at] = weighted
            total = total + weighted * normed
            scaled.append((normed * gain[:, at]).astype(BF16))
        dots[...] = total
        keys[...] += jnp.dot(
            jnp.concatenate(scaled, axis=1), rows, preferred_element_type=F32
        )
        return carry

    lax.fori_loop(0, count, block, 0)
    key_out[...] = keys[...].astype(BF16)
    mean = jnp.sum(dots[...], axis=-1, keepdims=True) / width

    def finish(i, carry):
        at = pl.ds(pl.multiple_of(i * 512, 512), 512)
        inv = inverse[:, :1]
        normed = hidden[:, at].astype(F32) * inv
        grad_hidden[:, at] = (inv * (grad[:, at] - normed * mean)).astype(BF16)
        return carry

    lax.fori_loop(0, width // 512, finish, 0)


def tail(place, hidden, gain, cotangent, inverse, weights):
    tokens, width = hidden.shape
    keys = cotangent.shape[1]
    count = len(weights)
    vmem = pl.BlockSpec(memory_space=pltpu.VMEM)
    return pl.pallas_call(
        functools.partial(tail_kernel, count),
        out_shape=(
            jax.ShapeDtypeStruct((tokens, keys), BF16),
            jax.ShapeDtypeStruct((tokens, width), BF16),
        ),
        in_specs=[pl.BlockSpec(memory_space=pltpu.SMEM)]
        + [vmem] * 4
        + [pl.BlockSpec(memory_space=pl.ANY)] * count,
        out_specs=(vmem, vmem),
        scratch_shapes=[
            pltpu.VMEM((count // 2, 2 * width // count, keys), BF16),
            pltpu.VMEM((tokens, width), F32),
            pltpu.VMEM((tokens, keys), F32),
            pltpu.VMEM((tokens, LANES), F32),
            pltpu.SemaphoreType.DMA((count // 2,)),
        ],
        compiler_params=pltpu.CompilerParams(vmem_limit_bytes=40 * 1024 * 1024),
        cost_estimate=pl.CostEstimate(
            flops=4 * tokens * width * keys, bytes_accessed=18 * 1024 * 1024, transcendentals=0
        ),
        name="tail",
    )(place, hidden, gain, cotangent, inverse, *weights)


def outer_step(current, moment, average):
    moment_new = 0.9 * moment + average
    return (current - 0.7 * (average + 0.9 * moment_new), moment_new)


def per_device(
    hidden_in,
    norm_gain,
    key_weight,
    key_cotangent,
    outer_params,
    outer_momentum,
    inner_params,
    fragment_index,
):
    hidden = hidden_in[0]
    cotangent = key_cotangent[0]
    own = key_weight[0]
    rows, width = own.shape
    cut = width // 2
    groups = SIZE["xh"], SIZE["y"], SIZE["z"]
    devices = groups[0] * groups[1] * groups[2]
    factor = float(hidden.shape[0] * devices) ** (-0.5)

    chosen = fragment_index[0]
    current = lax.dynamic_index_in_dim(outer_params, chosen, 0, keepdims=False)
    inner_now = lax.dynamic_index_in_dim(inner_params[0], chosen, 0, keepdims=False)
    part_a, part_b, inverse = weight_grad(hidden, norm_gain, cotangent)
    part_a = part_a.reshape(*groups, cut, rows)
    part_b = part_b.reshape(*groups, cut, rows)
    half = cut // 2

    mine = current - inner_now
    slabs = own.reshape(rows, -1, LANES).transpose(1, 0, 2)
    over_x = shift(slabs, "xh", 1)
    core = lax.ppermute(mine, "core", [(0, 1), (1, 0)])
    over_x, part_a, part_b, inverse, core = together(over_x, part_a, part_b, inverse, core)
    pair = jnp.concatenate([slabs, over_x], axis=1)

    sums = groups[0] * groups[1]

    def along_z(total, slab, step):
        moved = shift(jnp.concatenate([total.reshape(sums, cut, rows), slab]), "z", step)
        return moved[:sums], moved[sums:]

    far_b = term(part_b, "y", 1, 2)
    left, z7 = along_z(term(part_a, "z", 2, -4), pair, -1)
    right, z1 = along_z(term(part_a, "z", 2, 3), pair, 1)
    b_left = shift(far_b[..., half:, :], "y", -1)
    b_right = shift(far_b[..., :half, :], "y", 1)
    left, z7, right, z1, b_left, b_right = together(left, z7, right, z1, b_left, b_right)

    left, z6 = along_z(added(part_a, "z", 2, -3, left), z7, -1)
    right, z2 = along_z(added(part_a, "z", 2, 2, right), z1, 1)
    none = jnp.zeros_like(b_left)
    b_left = shift(
        added(part_b, "y", 1, -1, jnp.concatenate([none, b_left], axis=3)), "y", -1
    )
    b_right = shift(
        added(part_b, "y", 1, 1, jnp.concatenate([b_right, none], axis=3)), "y", 1
    )
    left, z6, right, z2 = together(left, z6, right, z2)

    left, z5 = along_z(added(part_a, "z", 2, -2, left), z6, -1)
    right, z3 = along_z(added(part_a, "z", 2, 1, right), z2, 1)
    first = jnp.concatenate([pair, z1, z7, z2, z6], axis=1)
    first1, first3 = shift(first, "y", 1), shift(first, "y", -1)
    left, z5, right, z3, b_left, b_right = together(left, z5, right, z3, b_left, b_right)

    sum_b = term(part_b, "y", 1, 0).astype(F32) + b_left.astype(F32) + b_right.astype(F32)
    sum_b = exchange_sum(sum_b.reshape(-1, cut, rows), ("xh", "z"))
    left = shift(added(part_a, "z", 2, -1, left), "z", -1)
    z4 = shift(z3, "z", 1)
    left, right, z4, first1, first3, core = together(left, right, z4, first1, first3, core)

    sum_a = term(part_a, "z", 2, 0).reshape(left.shape).astype(F32)
    sum_a = sum_a + left.astype(F32) + right.astype(F32)
    sum_a = exchange_sum(sum_a.reshape(-1, cut, rows), ("xh", "y"))
    second = jnp.concatenate([z3, z5, z4], axis=1)
    second1, second3 = shift(second, "y", 1), shift(second, "y", -1)
    first2 = shift(first1, "y", 1)
    both = mine + core
    summed = both + lax.ppermute(both, "xl", [(0, 1), (1, 0)])
    sum_a, sum_b, second1, second3, summed = together(sum_a, sum_b, second1, second3, summed)
    second2 = shift(second3, "y", -1)
    weights = [first, second, first1, second1, first2, second2, first3, second3]

    grad_weight = jnp.concatenate([sum_a.T, sum_b.T], axis=-1) * factor

    me = lax.axis_index(GROUP)
    own_gain = lax.dynamic_slice_in_dim(norm_gain[0], me * rows, rows)
    own_sum = jnp.sum(own.astype(F32) * grad_weight, axis=-1) / own_gain
    place = jnp.stack([lax.axis_index(axis) for axis in GROUP])
    grad_gain = lax.all_to_all(
        jnp.broadcast_to(own_sum[None], (devices, rows)), GROUP, 0, 0, tiled=True
    ).reshape(-1)
    key_out, grad_hidden = tail(place, hidden, norm_gain, cotangent, inverse, weights)

    moment = lax.dynamic_index_in_dim(outer_momentum, chosen, 0, keepdims=False)
    new_params, new_momentum = outer_step(current, moment, summed / 4.0)
    return (
        key_out[None],
        grad_weight[None],
        grad_hidden[None],
        grad_gain[None],
        new_params,
        new_momentum,
    )


def solution(mesh):
    fine = Mesh(mesh.devices.reshape(2, 2, 2, 4, 8), (*REPL, *GROUP))
    placed = (
        P(REPL, GROUP, None),
        P(REPL, None),
        P(REPL, GROUP, None),
        P(REPL, GROUP, None),
        P(None, GROUP, None),
        P(None, GROUP, None),
        P(REPL, None, GROUP, None),
        P(),
    )
    return jax.shard_map(
        per_device,
        mesh=fine,
        in_specs=placed,
        out_specs=(
            P(REPL, GROUP, None),
            P(REPL, GROUP, None),
            P(REPL, GROUP, None),
            P(REPL, None),
            P(GROUP, None),
            P(GROUP, None),
        ),
        check_vma=False,
    )
```

```python
import functools

import jax
import jax.numpy as jnp
from jax import lax
from jax.experimental import pallas as pl
from jax.experimental.pallas import tpu as pltpu
from jax.sharding import Mesh
from jax.sharding import PartitionSpec as P

GROUP = ("xh", "y", "z")
REPL = ("xl", "core")
SIZE = {"xh": 2, "y": 4, "z": 8}
BF16 = jnp.bfloat16
F32 = jnp.float32
LANES = 128
ORDER = (0, 1, 7, 2, 6, 3, 5, 4)


def shift(value, axis, step):
    n = SIZE[axis]
    return lax.ppermute(value, axis, [(i, (i + step) % n) for i in range(n)])


def together(*values):
    return lax.optimization_barrier(values)


def term(part, axis, dim, step):
    at = (lax.axis_index(axis) + step) & (SIZE[axis] - 1)
    return lax.dynamic_slice_in_dim(part, at, 1, dim)


def added(part, axis, dim, step, received):
    mine = term(part, axis, dim, step).reshape(received.shape)
    return (mine.astype(F32) + received.astype(F32)).astype(BF16)


def exchange_sum(part, axes):
    blocks = lax.all_to_all(part.astype(BF16), axes, 0, 0, tiled=True)
    return jnp.sum(blocks.astype(F32), axis=0)


def weight_grad_kernel(hidden, gain, cotangent, a_out, b_out, inv_out, inverse, turned):
    step = pl.program_id(0)
    tokens, width = hidden.shape
    blocks, cut, _ = a_out.shape
    span = blocks * LANES

    @pl.when(step == 0)
    def _():
        def add(i, total):
            piece = hidden[:, pl.ds(pl.multiple_of(i * 512, 512), 512)].astype(F32)
            square = piece * piece
            for j in range(4):
                total = total + square[:, j * LANES : (j + 1) * LANES]
            return total

        total = lax.fori_loop(0, width // 512, add, jnp.zeros((tokens, LANES), F32))
        mean = jnp.sum(total, axis=-1, keepdims=True) / width
        inverse[...] = jnp.broadcast_to(lax.rsqrt(mean + 1e-05), (tokens, LANES))
        inv_out[...] = inverse[...]
        turned[...] = cotangent[...].T

    for j in range(0, blocks, 2):
        at = pl.ds(pl.multiple_of(step * span + j * LANES, 2 * LANES), 2 * LANES)
        scaled = (hidden[:, at].astype(F32) * inverse[:, :1] * gain[:, at]).astype(BF16)
        both = jnp.dot(turned[...], scaled, preferred_element_type=F32)
        for i in range(2):
            lanes = slice(i * LANES, (i + 1) * LANES)
            a_out[j + i] = both[:cut, lanes].astype(BF16)
            b_out[j + i] = both[cut:, lanes].astype(BF16)


def weight_grad(hidden, gain, cotangent):
    tokens, width = hidden.shape
    keys = cotangent.shape[1]
    blocks, per_step, cut = width // LANES, 8, keys // 2
    whole = lambda i: (0, 0)
    part = jax.ShapeDtypeStruct((blocks, cut, LANES), BF16)
    return pl.pallas_call(
        weight_grad_kernel,
        grid=(blocks // per_step,),
        out_shape=(part, part, jax.ShapeDtypeStruct((tokens, LANES), F32)),
        in_specs=[
            pl.BlockSpec((tokens, width), whole),
            pl.BlockSpec((1, width), whole),
            pl.BlockSpec((tokens, keys), whole),
        ],
        out_specs=(
            pl.BlockSpec((per_step, cut, LANES), lambda i: (i, 0, 0)),
            pl.BlockSpec((per_step, cut, LANES), lambda i: (i, 0, 0)),
            pl.BlockSpec((tokens, LANES), whole),
        ),
        scratch_shapes=[pltpu.VMEM((tokens, LANES), F32), pltpu.VMEM((keys, tokens), BF16)],
        compiler_params=pltpu.CompilerParams(vmem_limit_bytes=56 * 1024 * 1024),
        cost_estimate=pl.CostEstimate(
            flops=2 * tokens * width * keys, bytes_accessed=22 * 1024 * 1024, transcendentals=0
        ),
        name="weight_grad",
    )(hidden, gain, cotangent)


def use_blocks(steps, place, hidden, gain, cotangent, inverse, weights, held, sems, keys, dots, keep):
    x, y, z = place[0], place[1], place[2]
    split = weights[0].shape[1]
    places = (pl.ds(0, split), pl.ds(split, weights[1].shape[1]))
    for i, ref in enumerate(weights):
        for group in range(ref.shape[0]):
            lanes = pl.ds(group * LANES, LANES)
            there = held.at[i // 2, places[i % 2], lanes]
            pltpu.make_async_copy(ref.at[group], there, sems.at[i // 2]).start()

    def block(i, carry):
        index, half = i // 2, i % 2

        @pl.when(half == 0)
        def _():
            pltpu.make_async_copy(held.at[index], held.at[index], sems.at[index]).wait()

        yr = steps[0]
        for k in range(1, len(steps)):
            yr = jnp.where(index == k, steps[k], yr)
        rows = held[index, pl.ds(pl.multiple_of(half * 1024, 1024), 1024), :]
        grads = lax.dot_general(
            cotangent[...], rows, (((1,), (1,)), ((), ())), preferred_element_type=F32
        )
        scaled = []
        total = dots[...]
        for j in range(8):
            zr = jnp.where(half == 0, ORDER[j // 2], ORDER[4 + j // 2])
            near = x ^ (j % 2), (y - yr) & 3, (z - zr) & 7
            feature = near[0] * 32 + near[1] * 8 + near[2]
            at = pl.ds(pl.multiple_of(feature * LANES, LANES), LANES)
            normed = hidden[:, at].astype(F32) * inverse[...]
            weighted = grads[:, j * LANES : (j + 1) * LANES] * gain[:, at]
            keep(feature, near, weighted)
            total = total + weighted * normed
            scaled.append((normed * gain[:, at]).astype(BF16))
        dots[...] = total
        keys[...] += jnp.dot(
            jnp.concatenate(scaled, axis=1), rows, preferred_element_type=F32
        )
        return carry

    lax.fori_loop(0, 2 * len(steps), block, 0)


def early_kernel(steps, place, hidden, gain, cotangent, inverse, *refs):
    count = 2 * len(steps)
    grad, keys, dots, held, sems = refs[count:]
    keys[...] = jnp.zeros_like(keys)
    dots[...] = jnp.zeros_like(dots)

    def keep(feature, near, weighted):
        grad[:, pl.ds(pl.multiple_of(feature * LANES, LANES), LANES)] = weighted

    use_blocks(
        steps, place, hidden, gain, cotangent, inverse, refs[:count], held, sems, keys, dots, keep
    )


def late_kernel(steps, place, hidden, gain, cotangent, inverse, grad, keys_in, dots_in, *refs):
    count = 2 * len(steps)
    key_out, grad_hidden, held, sems, keys, dots, fresh = refs[count:]
    width = hidden.shape[1]
    keys[...] = keys_in[...]
    dots[...] = dots_in[...]

    def keep(feature, near, weighted):
        at = (near[0] * 8 + near[2]) * LANES
        fresh[:, pl.ds(pl.multiple_of(at, LANES), LANES)] = weighted

    use_blocks(
        steps, place, hidden, gain, cotangent, inverse, refs[:count], held, sems, keys, dots, keep
    )
    key_out[...] = keys[...].astype(BF16)
    mean = jnp.sum(dots[...], axis=-1, keepdims=True) / width
    inv = inverse[:, :1]

    def result(at, weighted):
        normed = hidden[:, at].astype(F32) * inv
        grad_hidden[:, at] = (inv * (weighted - normed * mean)).astype(BF16)

    def early(i, carry):
        at = pl.ds(pl.multiple_of(i * 512, 512), 512)
        result(at, grad[:, at])
        return carry

    lax.fori_loop(0, width // 512, early, 0)

    def late(i, carry):
        y = (place[1] - steps[0]) & 3
        at = pl.ds(pl.multiple_of((i // 2) * 4096 + y * 1024 + (i % 2) * 512, 512), 512)
        result(at, fresh[:, pl.ds(pl.multiple_of(i * 512, 512), 512)])
        return carry

    lax.fori_loop(0, 4, late, 0)


def rows_call(kernel, steps, outs, scratch, operands, weights, name):
    hidden, cotangent = operands[1], operands[3]
    tokens, width = hidden.shape
    keys = cotangent.shape[1]
    vmem = pl.BlockSpec(memory_space=pltpu.VMEM)
    return pl.pallas_call(
        functools.partial(kernel, steps),
        out_shape=outs,
        in_specs=[pl.BlockSpec(memory_space=pltpu.SMEM)]
        + [vmem] * (len(operands) - 1)
        + [pl.BlockSpec(memory_space=pl.ANY)] * len(weights),
        out_specs=(vmem,) * len(outs),
        scratch_shapes=[
            pltpu.VMEM((len(steps), width // 4, keys), BF16),
            pltpu.SemaphoreType.DMA((len(steps),)),
            *scratch,
        ],
        compiler_params=pltpu.CompilerParams(vmem_limit_bytes=36 * 1024 * 1024),
        cost_estimate=pl.CostEstimate(
            flops=len(steps) * tokens * width * keys,
            bytes_accessed=(12 + 2 * len(steps)) * 1024 * 1024,
            transcendentals=0,
        ),
        name=name,
    )(*operands, *weights)


def outer_step(current, moment, average):
    moment_new = 0.9 * moment + average
    return (current - 0.7 * (average + 0.9 * moment_new), moment_new)


def per_device(
    hidden_in,
    norm_gain,
    key_weight,
    key_cotangent,
    outer_params,
    outer_momentum,
    inner_params,
    fragment_index,
):
    hidden = hidden_in[0]
    cotangent = key_cotangent[0]
    own = key_weight[0]
    rows, width = own.shape
    cut = width // 2
    groups = SIZE["xh"], SIZE["y"], SIZE["z"]
    devices = groups[0] * groups[1] * groups[2]
    factor = float(hidden.shape[0] * devices) ** (-0.5)

    chosen = fragment_index[0]
    current = lax.dynamic_index_in_dim(outer_params, chosen, 0, keepdims=False)
    inner_now = lax.dynamic_index_in_dim(inner_params[0], chosen, 0, keepdims=False)
    part_a, part_b, inverse = weight_grad(hidden, norm_gain, cotangent)
    part_a = part_a.reshape(*groups, cut, rows)
    part_b = part_b.reshape(*groups, cut, rows)
    half = cut // 2

    mine = current - inner_now
    slabs = own.reshape(rows, -1, LANES).transpose(1, 0, 2)
    over_x = shift(slabs, "xh", 1)
    core = lax.ppermute(mine, "core", [(0, 1), (1, 0)])
    over_x, part_a, part_b, inverse, core = together(over_x, part_a, part_b, inverse, core)
    pair = jnp.concatenate([slabs, over_x], axis=1)

    sums = groups[0] * groups[1]

    def along_z(total, slab, step):
        return shift(jnp.concatenate([total.reshape(sums, cut, rows), slab]), "z", step)

    far_b = term(part_b, "y", 1, 2)
    left = along_z(term(part_a, "z", 2, -4), pair, -1)
    right = along_z(term(part_a, "z", 2, 3), pair, 1)
    b_left = shift(far_b[..., half:, :], "y", -1)
    b_right = shift(far_b[..., :half, :], "y", 1)
    left, right, b_left, b_right = together(left, right, b_left, b_right)

    z7, z1 = left[sums:], right[sums:]
    left = along_z(added(part_a, "z", 2, -3, left[:sums]), z7, -1)
    right = along_z(added(part_a, "z", 2, 2, right[:sums]), z1, 1)
    none = jnp.zeros_like(b_left)
    b_left = shift(
        added(part_b, "y", 1, -1, jnp.concatenate([none, b_left], axis=3)), "y", -1
    )
    b_right = shift(
        added(part_b, "y", 1, 1, jnp.concatenate([b_right, none], axis=3)), "y", 1
    )
    left, right, b_left, b_right = together(left, right, b_left, b_right)

    z6, z2 = left[sums:], right[sums:]
    left = along_z(added(part_a, "z", 2, -2, left[:sums]), z6, -1)
    right = along_z(added(part_a, "z", 2, 1, right[:sums]), z2, 1)
    first = jnp.concatenate([pair, z1, z7, z2, z6], axis=1)
    first1, first3 = shift(first, "y", 1), shift(first, "y", -1)
    sum_b = term(part_b, "y", 1, 0).astype(F32) + b_left.astype(F32) + b_right.astype(F32)
    sum_b = exchange_sum(sum_b.reshape(-1, cut, rows), ("xh", "z"))
    left, right, first1, first3, sum_b, core = together(
        left, right, first1, first3, sum_b, core
    )

    z5, z3 = left[sums:], right[sums:]
    left = shift(added(part_a, "z", 2, -1, left[:sums]), "z", -1)
    z4 = shift(z3, "z", 1)
    first2 = shift(first1, "y", 1)
    both = mine + core
    summed = both + lax.ppermute(both, "xl", [(0, 1), (1, 0)])
    left, right, z4, summed = together(left, right, z4, summed)

    second = jnp.concatenate([z3, z5, z4], axis=1)
    second1, second3 = shift(second, "y", 1), shift(second, "y", -1)
    sum_a = term(part_a, "z", 2, 0).reshape(left.shape).astype(F32)
    sum_a = sum_a + left.astype(F32) + right[:sums].astype(F32)
    sum_a = exchange_sum(sum_a.reshape(-1, cut, rows), ("xh", "y"))
    sum_a, sum_b, second1, second3 = together(sum_a, sum_b, second1, second3)
    second2 = shift(second3, "y", -1)

    grad_weight = jnp.concatenate([sum_a.T, sum_b.T], axis=-1) * factor

    me = lax.axis_index(GROUP)
    own_gain = lax.dynamic_slice_in_dim(norm_gain[0], me * rows, rows)
    own_sum = jnp.sum(own.astype(F32) * grad_weight, axis=-1) / own_gain
    place = jnp.stack([lax.axis_index(axis) for axis in GROUP])
    grad_gain = lax.all_to_all(
        jnp.broadcast_to(own_sum[None], (devices, rows)), GROUP, 0, 0, tiled=True
    ).reshape(-1)
    keys = cotangent.shape[1]
    tokens, features = hidden.shape
    operands = (place, hidden, norm_gain, cotangent, inverse)
    partial = rows_call(
        early_kernel,
        (0, 1, 3),
        (
            jax.ShapeDtypeStruct((tokens, features), F32),
            jax.ShapeDtypeStruct((tokens, keys), F32),
            jax.ShapeDtypeStruct((tokens, LANES), F32),
        ),
        (),
        operands,
        (first, second, first1, second1, first3, second3),
        "early_rows",
    )
    key_out, grad_hidden = rows_call(
        late_kernel,
        (2,),
        (
            jax.ShapeDtypeStruct((tokens, keys), BF16),
            jax.ShapeDtypeStruct((tokens, features), BF16),
        ),
        (
            pltpu.VMEM((tokens, keys), F32),
            pltpu.VMEM((tokens, LANES), F32),
            pltpu.VMEM((tokens, features // 4), F32),
        ),
        (*operands, *partial),
        (first2, second2),
        "late_rows",
    )

    moment = lax.dynamic_index_in_dim(outer_momentum, chosen, 0, keepdims=False)
    new_params, new_momentum = outer_step(current, moment, summed / 4.0)
    return (
        key_out[None],
        grad_weight[None],
        grad_hidden[None],
        grad_gain[None],
        new_params,
        new_momentum,
    )


def solution(mesh):
    fine = Mesh(mesh.devices.reshape(2, 2, 2, 4, 8), (*REPL, *GROUP))
    placed = (
        P(REPL, GROUP, None),
        P(REPL, None),
        P(REPL, GROUP, None),
        P(REPL, GROUP, None),
        P(None, GROUP, None),
        P(None, GROUP, None),
        P(REPL, None, GROUP, None),
        P(),
    )
    return jax.shard_map(
        per_device,
        mesh=fine,
        in_specs=placed,
        out_specs=(
            P(REPL, GROUP, None),
            P(REPL, GROUP, None),
            P(REPL, GROUP, None),
            P(REPL, None),
            P(GROUP, None),
            P(GROUP, None),
        ),
        check_vma=False,
    )
```

```python
import functools

import jax
import jax.numpy as jnp
from jax import lax
from jax.experimental import pallas as pl
from jax.experimental.pallas import tpu as pltpu
from jax.sharding import Mesh
from jax.sharding import PartitionSpec as P

GROUP = ("xh", "y", "z")
REPL = ("xl", "core")
SIZE = {"xh": 2, "y": 4, "z": 8}
BF16 = jnp.bfloat16
F32 = jnp.float32
LANES = 128
ORDER = (0, 1, 7, 2, 6, 3, 5, 4)


def shift(value, axis, step):
    n = SIZE[axis]
    return lax.ppermute(value, axis, [(i, (i + step) % n) for i in range(n)])


def together(*values):
    return lax.optimization_barrier(values)


def term(part, axis, dim, step):
    at = (lax.axis_index(axis) + step) & (SIZE[axis] - 1)
    return lax.dynamic_slice_in_dim(part, at, 1, dim)


def added(part, axis, dim, step, received):
    mine = term(part, axis, dim, step).reshape(received.shape)
    return (mine.astype(F32) + received.astype(F32)).astype(BF16)


def exchange_sum(part, axes):
    blocks = lax.all_to_all(part.astype(BF16), axes, 0, 0, tiled=True)
    return jnp.sum(blocks.astype(F32), axis=0)


def weight_grad_kernel(hidden, gain, cotangent, a_out, b_out, inv_out, inverse, turned):
    step = pl.program_id(0)
    tokens, width = hidden.shape
    blocks, cut, _ = a_out.shape
    span = blocks * LANES

    @pl.when(step == 0)
    def _():
        def add(i, total):
            piece = hidden[:, pl.ds(pl.multiple_of(i * 512, 512), 512)].astype(F32)
            square = piece * piece
            for j in range(4):
                total = total + square[:, j * LANES : (j + 1) * LANES]
            return total

        total = lax.fori_loop(0, width // 512, add, jnp.zeros((tokens, LANES), F32))
        mean = jnp.sum(total, axis=-1, keepdims=True) / width
        inverse[...] = jnp.broadcast_to(lax.rsqrt(mean + 1e-05), (tokens, LANES))
        inv_out[...] = inverse[...]
        turned[...] = cotangent[...].T

    for j in range(0, blocks, 2):
        at = pl.ds(pl.multiple_of(step * span + j * LANES, 2 * LANES), 2 * LANES)
        scaled = (hidden[:, at].astype(F32) * inverse[:, :1] * gain[:, at]).astype(BF16)
        both = jnp.dot(turned[...], scaled, preferred_element_type=F32)
        for i in range(2):
            lanes = slice(i * LANES, (i + 1) * LANES)
            a_out[j + i] = both[:cut, lanes].astype(BF16)
            b_out[j + i] = both[cut:, lanes].astype(BF16)


def weight_grad(hidden, gain, cotangent):
    tokens, width = hidden.shape
    keys = cotangent.shape[1]
    blocks, per_step, cut = width // LANES, 8, keys // 2
    whole = lambda i: (0, 0)
    part = jax.ShapeDtypeStruct((blocks, cut, LANES), BF16)
    return pl.pallas_call(
        weight_grad_kernel,
        grid=(blocks // per_step,),
        out_shape=(part, part, jax.ShapeDtypeStruct((tokens, LANES), F32)),
        in_specs=[
            pl.BlockSpec((tokens, width), whole),
            pl.BlockSpec((1, width), whole),
            pl.BlockSpec((tokens, keys), whole),
        ],
        out_specs=(
            pl.BlockSpec((per_step, cut, LANES), lambda i: (i, 0, 0)),
            pl.BlockSpec((per_step, cut, LANES), lambda i: (i, 0, 0)),
            pl.BlockSpec((tokens, LANES), whole),
        ),
        scratch_shapes=[pltpu.VMEM((tokens, LANES), F32), pltpu.VMEM((keys, tokens), BF16)],
        compiler_params=pltpu.CompilerParams(vmem_limit_bytes=56 * 1024 * 1024),
        cost_estimate=pl.CostEstimate(
            flops=2 * tokens * width * keys, bytes_accessed=22 * 1024 * 1024, transcendentals=0
        ),
        name="weight_grad",
    )(hidden, gain, cotangent)


def use_blocks(steps, place, hidden, gain, cotangent, inverse, weights, held, sems, keys, dots, keep):
    x, y, z = place[0], place[1], place[2]
    split = weights[0].shape[1]
    places = (pl.ds(0, split), pl.ds(split, weights[1].shape[1]))
    for i, ref in enumerate(weights):
        for group in range(ref.shape[0]):
            lanes = pl.ds(group * LANES, LANES)
            there = held.at[i // 2, places[i % 2], lanes]
            pltpu.make_async_copy(ref.at[group], there, sems.at[i // 2]).start()

    def block(i, carry):
        index, half = i // 2, i % 2

        @pl.when(half == 0)
        def _():
            pltpu.make_async_copy(held.at[index], held.at[index], sems.at[index]).wait()

        yr = steps[0]
        for k in range(1, len(steps)):
            yr = jnp.where(index == k, steps[k], yr)
        rows = held[index, pl.ds(pl.multiple_of(half * 1024, 1024), 1024), :]
        grads = lax.dot_general(
            cotangent[...], rows, (((1,), (1,)), ((), ())), preferred_element_type=F32
        )
        scaled = []
        total = dots[...]
        for j in range(8):
            zr = jnp.where(half == 0, ORDER[j // 2], ORDER[4 + j // 2])
            near = x ^ (j % 2), (y - yr) & 3, (z - zr) & 7
            feature = near[0] * 32 + near[1] * 8 + near[2]
            at = pl.ds(pl.multiple_of(feature * LANES, LANES), LANES)
            normed = hidden[:, at].astype(F32) * inverse[...]
            weighted = grads[:, j * LANES : (j + 1) * LANES] * gain[:, at]
            keep(feature, near, weighted)
            total = total + weighted * normed
            scaled.append((normed * gain[:, at]).astype(BF16))
        dots[...] = total
        keys[...] += jnp.dot(
            jnp.concatenate(scaled, axis=1), rows, preferred_element_type=F32
        )
        return carry

    lax.fori_loop(0, 2 * len(steps), block, 0)


def early_kernel(steps, place, hidden, gain, cotangent, inverse, *refs):
    count = 2 * len(steps)
    grad, keys, dots, held, sems = refs[count:]
    keys[...] = jnp.zeros_like(keys)
    dots[...] = jnp.zeros_like(dots)

    def keep(feature, near, weighted):
        grad[:, pl.ds(pl.multiple_of(feature * LANES, LANES), LANES)] = weighted

    use_blocks(
        steps, place, hidden, gain, cotangent, inverse, refs[:count], held, sems, keys, dots, keep
    )


def late_kernel(steps, place, hidden, gain, cotangent, inverse, grad, keys_in, dots_in, after, *refs):
    count = 2 * len(steps)
    del after
    key_out, grad_hidden, held, sems, keys, dots, fresh = refs[count:]
    width = hidden.shape[1]
    keys[...] = keys_in[...]
    dots[...] = dots_in[...]

    def keep(feature, near, weighted):
        at = (near[0] * 8 + near[2]) * LANES
        fresh[:, pl.ds(pl.multiple_of(at, LANES), LANES)] = weighted

    use_blocks(
        steps, place, hidden, gain, cotangent, inverse, refs[:count], held, sems, keys, dots, keep
    )
    key_out[...] = keys[...].astype(BF16)
    mean = jnp.sum(dots[...], axis=-1, keepdims=True) / width
    inv = inverse[:, :1]

    def result(at, weighted):
        normed = hidden[:, at].astype(F32) * inv
        grad_hidden[:, at] = (inv * (weighted - normed * mean)).astype(BF16)

    def early(i, carry):
        at = pl.ds(pl.multiple_of(i * 512, 512), 512)
        result(at, grad[:, at])
        return carry

    lax.fori_loop(0, width // 512, early, 0)

    def late(i, carry):
        y = (place[1] - steps[0]) & 3
        at = pl.ds(pl.multiple_of((i // 2) * 4096 + y * 1024 + (i % 2) * 512, 512), 512)
        result(at, fresh[:, pl.ds(pl.multiple_of(i * 512, 512), 512)])
        return carry

    lax.fori_loop(0, 4, late, 0)


def rows_call(kernel, steps, outs, scratch, operands, weights, name):
    hidden, cotangent = operands[1], operands[3]
    tokens, width = hidden.shape
    keys = cotangent.shape[1]
    vmem = pl.BlockSpec(memory_space=pltpu.VMEM)
    return pl.pallas_call(
        functools.partial(kernel, steps),
        out_shape=outs,
        in_specs=[pl.BlockSpec(memory_space=pltpu.SMEM)]
        + [vmem] * (len(operands) - 1)
        + [pl.BlockSpec(memory_space=pl.ANY)] * len(weights),
        out_specs=(vmem,) * len(outs),
        scratch_shapes=[
            pltpu.VMEM((len(steps), width // 4, keys), BF16),
            pltpu.SemaphoreType.DMA((len(steps),)),
            *scratch,
        ],
        compiler_params=pltpu.CompilerParams(vmem_limit_bytes=60 * 1024 * 1024),
        cost_estimate=pl.CostEstimate(
            flops=len(steps) * tokens * width * keys,
            bytes_accessed=(12 + 2 * len(steps)) * 1024 * 1024,
            transcendentals=0,
        ),
        name=name,
    )(*operands, *weights)


def outer_step(current, moment, average):
    moment_new = 0.9 * moment + average
    return (current - 0.7 * (average + 0.9 * moment_new), moment_new)


def per_device(
    hidden_in,
    norm_gain,
    key_weight,
    key_cotangent,
    outer_params,
    outer_momentum,
    inner_params,
    fragment_index,
):
    hidden = hidden_in[0]
    cotangent = key_cotangent[0]
    own = key_weight[0]
    rows, width = own.shape
    cut = width // 2
    groups = SIZE["xh"], SIZE["y"], SIZE["z"]
    devices = groups[0] * groups[1] * groups[2]
    factor = float(hidden.shape[0] * devices) ** (-0.5)

    chosen = fragment_index[0]
    current = lax.dynamic_index_in_dim(outer_params, chosen, 0, keepdims=False)
    inner_now = lax.dynamic_index_in_dim(inner_params[0], chosen, 0, keepdims=False)
    part_a, part_b, inverse = weight_grad(hidden, norm_gain, cotangent)
    part_a = part_a.reshape(*groups, cut, rows)
    part_b = part_b.reshape(*groups, cut, rows)
    half = cut // 2

    mine = current - inner_now
    slabs = own.reshape(rows, -1, LANES).transpose(1, 0, 2)
    over_x = shift(slabs, "xh", 1)
    core = lax.ppermute(mine, "core", [(0, 1), (1, 0)])
    over_x, part_a, part_b, inverse, core = together(over_x, part_a, part_b, inverse, core)
    pair = jnp.concatenate([slabs, over_x], axis=1)

    sums = groups[0] * groups[1]

    def along_z(total, slab, step):
        return shift(jnp.concatenate([total.reshape(sums, cut, rows), slab]), "z", step)

    far_b = term(part_b, "y", 1, 2)
    left = along_z(term(part_a, "z", 2, -4), pair, -1)
    right = along_z(term(part_a, "z", 2, 3), pair, 1)
    b_left = shift(far_b[..., half:, :], "y", -1)
    b_right = shift(far_b[..., :half, :], "y", 1)
    left, right, b_left, b_right = together(left, right, b_left, b_right)

    z7, z1 = left[sums:], right[sums:]
    left = along_z(added(part_a, "z", 2, -3, left[:sums]), z7, -1)
    right = along_z(added(part_a, "z", 2, 2, right[:sums]), z1, 1)
    none = jnp.zeros_like(b_left)
    b_left = shift(
        added(part_b, "y", 1, -1, jnp.concatenate([none, b_left], axis=3)), "y", -1
    )
    b_right = shift(
        added(part_b, "y", 1, 1, jnp.concatenate([b_right, none], axis=3)), "y", 1
    )
    left, right, b_left, b_right = together(left, right, b_left, b_right)

    z6, z2 = left[sums:], right[sums:]
    left = along_z(added(part_a, "z", 2, -2, left[:sums]), z6, -1)
    right = along_z(added(part_a, "z", 2, 1, right[:sums]), z2, 1)
    first = jnp.concatenate([pair, z1, z7, z2, z6], axis=1)
    first1, first3 = shift(first, "y", 1), shift(first, "y", -1)
    left, right = together(left, right)

    z5, z3 = left[sums:], right[sums:]
    left = shift(added(part_a, "z", 2, -1, left[:sums]), "z", -1)
    z4 = shift(z3, "z", 1)
    left, right, z4, first1, first3, b_left, b_right, core = together(
        left, right, z4, first1, first3, b_left, b_right, core
    )

    second = jnp.concatenate([z3, z5, z4], axis=1)
    second1, second3 = shift(second, "y", 1), shift(second, "y", -1)
    sum_a = term(part_a, "z", 2, 0).reshape(left.shape).astype(F32)
    sum_a = sum_a + left.astype(F32) + right[:sums].astype(F32)
    sum_a = exchange_sum(sum_a.reshape(-1, cut, rows), ("xh", "y"))
    sum_b = term(part_b, "y", 1, 0).astype(F32) + b_left.astype(F32) + b_right.astype(F32)
    sum_b = sum_b.reshape(-1, cut, rows).astype(BF16)
    first2 = shift(first1, "y", 1)
    sum_a, sum_b, second1, second3, core = together(sum_a, sum_b, second1, second3, core)

    second2 = shift(second3, "y", -1)
    both = mine + core
    summed = both + lax.ppermute(both, "xl", [(0, 1), (1, 0)])
    sum_b = exchange_sum(sum_b, ("xh", "z"))
    sum_b, summed = together(sum_b, summed)

    grad_weight = jnp.concatenate([sum_a.T, sum_b.T], axis=-1) * factor

    me = lax.axis_index(GROUP)
    own_gain = lax.dynamic_slice_in_dim(norm_gain[0], me * rows, rows)
    own_sum = jnp.sum(own.astype(F32) * grad_weight, axis=-1) / own_gain
    place = jnp.stack([lax.axis_index(axis) for axis in GROUP])
    place = jnp.stack([lax.axis_index(axis) for axis in GROUP])
    grad_gain = lax.all_to_all(
        jnp.broadcast_to(own_sum[None], (devices, rows)), GROUP, 0, 0, tiled=True
    ).reshape(-1)
    keys = cotangent.shape[1]
    tokens, features = hidden.shape
    operands = (place, hidden, norm_gain, cotangent, inverse)
    partial = rows_call(
        early_kernel,
        (0, 1, 3),
        (
            jax.ShapeDtypeStruct((tokens, features), F32),
            jax.ShapeDtypeStruct((tokens, keys), F32),
            jax.ShapeDtypeStruct((tokens, LANES), F32),
        ),
        (),
        operands,
        (first, second, first1, second1, first3, second3),
        "early_rows",
    )

    key_out, grad_hidden = rows_call(
        late_kernel,
        (2,),
        (
            jax.ShapeDtypeStruct((tokens, keys), BF16),
            jax.ShapeDtypeStruct((tokens, features), BF16),
        ),
        (
            pltpu.VMEM((tokens, keys), F32),
            pltpu.VMEM((tokens, LANES), F32),
            pltpu.VMEM((tokens, features // 4), F32),
        ),
        (*operands, *partial, own_sum[None]),
        (first2, second2),
        "late_rows",
    )

    moment = lax.dynamic_index_in_dim(outer_momentum, chosen, 0, keepdims=False)
    new_params, new_momentum = outer_step(current, moment, summed / 4.0)
    return (
        key_out[None],
        grad_weight[None],
        grad_hidden[None],
        grad_gain[None],
        new_params,
        new_momentum,
    )


def solution(mesh):
    fine = Mesh(mesh.devices.reshape(2, 2, 2, 4, 8), (*REPL, *GROUP))
    placed = (
        P(REPL, GROUP, None),
        P(REPL, None),
        P(REPL, GROUP, None),
        P(REPL, GROUP, None),
        P(None, GROUP, None),
        P(None, GROUP, None),
        P(REPL, None, GROUP, None),
        P(),
    )
    return jax.shard_map(
        per_device,
        mesh=fine,
        in_specs=placed,
        out_specs=(
            P(REPL, GROUP, None),
            P(REPL, GROUP, None),
            P(REPL, GROUP, None),
            P(REPL, None),
            P(GROUP, None),
            P(GROUP, None),
        ),
        check_vma=False,
    )
```

```python
import functools

import jax
import jax.numpy as jnp
from jax import lax
from jax.experimental import pallas as pl
from jax.experimental.pallas import tpu as pltpu
from jax.sharding import Mesh
from jax.sharding import PartitionSpec as P

GROUP = ("xh", "y", "z")
REPL = ("xl", "core")
SIZE = {"xh": 2, "y": 4, "z": 8}
BF16 = jnp.bfloat16
F32 = jnp.float32
LANES = 128
ORDER = (0, 1, 7, 2, 6, 3, 5, 4)


def shift(value, axis, step):
    n = SIZE[axis]
    return lax.ppermute(value, axis, [(i, (i + step) % n) for i in range(n)])


def together(*values):
    return lax.optimization_barrier(values)


def term(part, axis, dim, step):
    at = (lax.axis_index(axis) + step) & (SIZE[axis] - 1)
    return lax.dynamic_slice_in_dim(part, at, 1, dim)


def added(part, axis, dim, step, received):
    mine = term(part, axis, dim, step).reshape(received.shape)
    return (mine.astype(F32) + received.astype(F32)).astype(BF16)


def exchange_sum(part, axes):
    blocks = lax.all_to_all(part.astype(BF16), axes, 0, 0, tiled=True)
    return jnp.sum(blocks.astype(F32), axis=0)


def weight_grad_kernel(hidden, gain, cotangent, a_out, b_out, inv_out, inverse, turned):
    step = pl.program_id(0)
    tokens, width = hidden.shape
    blocks, cut, _ = a_out.shape
    span = blocks * LANES

    @pl.when(step == 0)
    def _():
        def add(i, total):
            piece = hidden[:, pl.ds(pl.multiple_of(i * 512, 512), 512)].astype(F32)
            square = piece * piece
            for j in range(4):
                total = total + square[:, j * LANES : (j + 1) * LANES]
            return total

        total = lax.fori_loop(0, width // 512, add, jnp.zeros((tokens, LANES), F32))
        mean = jnp.sum(total, axis=-1, keepdims=True) / width
        inverse[...] = jnp.broadcast_to(lax.rsqrt(mean + 1e-05), (tokens, LANES))
        inv_out[...] = inverse[...]
        turned[...] = cotangent[...].T

    for j in range(0, blocks, 2):
        at = pl.ds(pl.multiple_of(step * span + j * LANES, 2 * LANES), 2 * LANES)
        scaled = (hidden[:, at].astype(F32) * inverse[:, :1] * gain[:, at]).astype(BF16)
        both = jnp.dot(turned[...], scaled, preferred_element_type=F32)
        for i in range(2):
            lanes = slice(i * LANES, (i + 1) * LANES)
            a_out[j + i] = both[:cut, lanes].astype(BF16)
            b_out[j + i] = both[cut:, lanes].astype(BF16)


def weight_grad(hidden, gain, cotangent):
    tokens, width = hidden.shape
    keys = cotangent.shape[1]
    blocks, per_step, cut = width // LANES, 8, keys // 2
    whole = lambda i: (0, 0)
    part = jax.ShapeDtypeStruct((blocks, cut, LANES), BF16)
    return pl.pallas_call(
        weight_grad_kernel,
        grid=(blocks // per_step,),
        out_shape=(part, part, jax.ShapeDtypeStruct((tokens, LANES), F32)),
        in_specs=[
            pl.BlockSpec((tokens, width), whole),
            pl.BlockSpec((1, width), whole),
            pl.BlockSpec((tokens, keys), whole),
        ],
        out_specs=(
            pl.BlockSpec((per_step, cut, LANES), lambda i: (i, 0, 0)),
            pl.BlockSpec((per_step, cut, LANES), lambda i: (i, 0, 0)),
            pl.BlockSpec((tokens, LANES), whole),
        ),
        scratch_shapes=[pltpu.VMEM((tokens, LANES), F32), pltpu.VMEM((keys, tokens), BF16)],
        compiler_params=pltpu.CompilerParams(vmem_limit_bytes=56 * 1024 * 1024),
        cost_estimate=pl.CostEstimate(
            flops=2 * tokens * width * keys, bytes_accessed=22 * 1024 * 1024, transcendentals=0
        ),
        name="weight_grad",
    )(hidden, gain, cotangent)


def use_blocks(steps, place, hidden, gain, cotangent, inverse, weights, held, sems, keys, dots, keep):
    x, y, z = place[0], place[1], place[2]
    split = weights[0].shape[1]
    places = (pl.ds(0, split), pl.ds(split, weights[1].shape[1]))
    for i, ref in enumerate(weights):
        for group in range(ref.shape[0]):
            lanes = pl.ds(group * LANES, LANES)
            there = held.at[i // 2, places[i % 2], lanes]
            pltpu.make_async_copy(ref.at[group], there, sems.at[i // 2]).start()

    def block(i, carry):
        index, half = i // 2, i % 2

        @pl.when(half == 0)
        def _():
            pltpu.make_async_copy(held.at[index], held.at[index], sems.at[index]).wait()

        yr = steps[0]
        for k in range(1, len(steps)):
            yr = jnp.where(index == k, steps[k], yr)
        rows = held[index, pl.ds(pl.multiple_of(half * 1024, 1024), 1024), :]
        grads = lax.dot_general(
            cotangent[...], rows, (((1,), (1,)), ((), ())), preferred_element_type=F32
        )
        scaled = []
        total = dots[...]
        for j in range(8):
            zr = jnp.where(half == 0, ORDER[j // 2], ORDER[4 + j // 2])
            near = x ^ (j % 2), (y - yr) & 3, (z - zr) & 7
            feature = near[0] * 32 + near[1] * 8 + near[2]
            at = pl.ds(pl.multiple_of(feature * LANES, LANES), LANES)
            normed = hidden[:, at].astype(F32) * inverse[...]
            weighted = grads[:, j * LANES : (j + 1) * LANES] * gain[:, at]
            keep(feature, near, weighted)
            total = total + weighted * normed
            scaled.append((normed * gain[:, at]).astype(BF16))
        dots[...] = total
        keys[...] += jnp.dot(
            jnp.concatenate(scaled, axis=1), rows, preferred_element_type=F32
        )
        return carry

    lax.fori_loop(0, 2 * len(steps), block, 0)


def early_kernel(steps, place, hidden, gain, cotangent, inverse, *refs):
    count = 2 * len(steps)
    grad, keys, dots, held, sems = refs[count:]
    keys[...] = jnp.zeros_like(keys)
    dots[...] = jnp.zeros_like(dots)

    def keep(feature, near, weighted):
        grad[:, pl.ds(pl.multiple_of(feature * LANES, LANES), LANES)] = weighted

    use_blocks(
        steps, place, hidden, gain, cotangent, inverse, refs[:count], held, sems, keys, dots, keep
    )


def late_kernel(steps, place, hidden, gain, cotangent, inverse, keys_in, dots_in, after, *refs):
    del after
    grad_hbm, weights = refs[0], refs[1 : 1 + 2 * len(steps)]
    outs = refs[1 + 2 * len(steps) :]
    key_out, grad_hidden, held, sems, keys, dots, fresh, grad, done, load_sem, store_sems = outs
    width = hidden.shape[1]
    load = pltpu.make_async_copy(grad_hbm, grad, load_sem)
    load.start()
    keys[...] = keys_in[...]
    dots[...] = dots_in[...]

    def keep(feature, near, weighted):
        at = (near[0] * 8 + near[2]) * LANES
        fresh[:, pl.ds(pl.multiple_of(at, LANES), LANES)] = weighted

    use_blocks(
        steps, place, hidden, gain, cotangent, inverse, weights, held, sems, keys, dots, keep
    )
    key_out[...] = keys[...].astype(BF16)
    mean = jnp.sum(dots[...], axis=-1, keepdims=True) / width
    inv = inverse[:, :1]
    y = (place[1] - steps[0]) & 3
    load.wait()

    stores = []
    for quarter in range(4):

        def finish(i, carry, quarter=quarter):
            part = quarter * 4 + i
            at = pl.ds(pl.multiple_of(part * 512, 512), 512)
            here = (part // 8) * 1024 + (part % 2) * 512
            new = fresh[:, pl.ds(pl.multiple_of(here, 512), 512)]
            weighted = jnp.where((part // 2) % 4 == y, new, grad[:, at])
            normed = hidden[:, at].astype(F32) * inv
            lanes = pl.ds(pl.multiple_of(i * 512, 512), 512)
            done[quarter, :, lanes] = (inv * (weighted - normed * mean)).astype(BF16)
            return carry

        lax.fori_loop(0, 4, finish, 0)
        there = grad_hidden.at[:, pl.ds(quarter * 2048, 2048)]
        stores.append(pltpu.make_async_copy(done.at[quarter], there, store_sems.at[quarter]))
        stores[-1].start()
    for store in stores:
        store.wait()


def rows_call(kernel, steps, outs, out_specs, scratch, operands, weights, name):
    hidden, cotangent = operands[1], operands[3]
    tokens, width = hidden.shape
    keys = cotangent.shape[1]
    vmem = pl.BlockSpec(memory_space=pltpu.VMEM)
    return pl.pallas_call(
        functools.partial(kernel, steps),
        out_shape=outs,
        in_specs=[pl.BlockSpec(memory_space=pltpu.SMEM)]
        + [vmem] * (len(operands) - 1)
        + [pl.BlockSpec(memory_space=pl.ANY)] * len(weights),
        out_specs=out_specs,
        scratch_shapes=[
            pltpu.VMEM((len(steps), width // 4, keys), BF16),
            pltpu.SemaphoreType.DMA((len(steps),)),
            *scratch,
        ],
        compiler_params=pltpu.CompilerParams(vmem_limit_bytes=60 * 1024 * 1024),
        cost_estimate=pl.CostEstimate(
            flops=len(steps) * tokens * width * keys,
            bytes_accessed=(12 + 2 * len(steps)) * 1024 * 1024,
            transcendentals=0,
        ),
        name=name,
    )(*operands, *weights)


def outer_step(current, moment, average):
    moment_new = 0.9 * moment + average
    return (current - 0.7 * (average + 0.9 * moment_new), moment_new)


def per_device(
    hidden_in,
    norm_gain,
    key_weight,
    key_cotangent,
    outer_params,
    outer_momentum,
    inner_params,
    fragment_index,
):
    hidden = hidden_in[0]
    cotangent = key_cotangent[0]
    own = key_weight[0]
    rows, width = own.shape
    cut = width // 2
    groups = SIZE["xh"], SIZE["y"], SIZE["z"]
    devices = groups[0] * groups[1] * groups[2]
    factor = float(hidden.shape[0] * devices) ** (-0.5)

    chosen = fragment_index[0]
    current = lax.dynamic_index_in_dim(outer_params, chosen, 0, keepdims=False)
    inner_now = lax.dynamic_index_in_dim(inner_params[0], chosen, 0, keepdims=False)
    part_a, part_b, inverse = weight_grad(hidden, norm_gain, cotangent)
    part_a = part_a.reshape(*groups, cut, rows)
    part_b = part_b.reshape(*groups, cut, rows)
    half = cut // 2

    mine = current - inner_now
    slabs = own.reshape(rows, -1, LANES).transpose(1, 0, 2)
    over_x = shift(slabs, "xh", 1)
    core = lax.ppermute(mine, "core", [(0, 1), (1, 0)])
    over_x, part_a, part_b, inverse, core = together(over_x, part_a, part_b, inverse, core)
    pair = jnp.concatenate([slabs, over_x], axis=1)

    sums = groups[0] * groups[1]

    def along_z(total, slab, step):
        return shift(jnp.concatenate([total.reshape(sums, cut, rows), slab]), "z", step)

    far_b = term(part_b, "y", 1, 2)
    left = along_z(term(part_a, "z", 2, -4), pair, -1)
    right = along_z(term(part_a, "z", 2, 3), pair, 1)
    b_left = shift(far_b[..., half:, :], "y", -1)
    b_right = shift(far_b[..., :half, :], "y", 1)
    left, right, b_left, b_right = together(left, right, b_left, b_right)

    z7, z1 = left[sums:], right[sums:]
    left = along_z(added(part_a, "z", 2, -3, left[:sums]), z7, -1)
    right = along_z(added(part_a, "z", 2, 2, right[:sums]), z1, 1)
    none = jnp.zeros_like(b_left)
    b_left = shift(
        added(part_b, "y", 1, -1, jnp.concatenate([none, b_left], axis=3)), "y", -1
    )
    b_right = shift(
        added(part_b, "y", 1, 1, jnp.concatenate([b_right, none], axis=3)), "y", 1
    )
    left, right, b_left, b_right = together(left, right, b_left, b_right)

    z6, z2 = left[sums:], right[sums:]
    left = along_z(added(part_a, "z", 2, -2, left[:sums]), z6, -1)
    right = along_z(added(part_a, "z", 2, 1, right[:sums]), z2, 1)
    first = jnp.concatenate([pair, z1, z7, z2, z6], axis=1)
    first1, first3 = shift(first, "y", 1), shift(first, "y", -1)
    left, right = together(left, right)

    z5, z3 = left[sums:], right[sums:]
    left = shift(added(part_a, "z", 2, -1, left[:sums]), "z", -1)
    z4 = shift(z3, "z", 1)
    sum_b = term(part_b, "y", 1, 0).astype(F32) + b_left.astype(F32) + b_right.astype(F32)
    sum_b = exchange_sum(sum_b.reshape(-1, cut, rows), ("xh", "z"))
    left, right, z4, first1, first3, core = together(left, right, z4, first1, first3, core)

    second = jnp.concatenate([z3, z5, z4], axis=1)
    second1, second3 = shift(second, "y", 1), shift(second, "y", -1)
    both = mine + core
    summed = both + lax.ppermute(both, "xl", [(0, 1), (1, 0)])
    moment = lax.dynamic_index_in_dim(outer_momentum, chosen, 0, keepdims=False)
    new_params, new_momentum = outer_step(current, moment, summed / 4.0)
    sum_a = term(part_a, "z", 2, 0).reshape(left.shape).astype(F32)
    sum_a = sum_a + left.astype(F32) + right[:sums].astype(F32)
    sum_a = sum_a.reshape(-1, cut, rows).astype(BF16)
    first2 = shift(first1, "y", 1)
    sum_a, sum_b, second1, second3, new_params, new_momentum = together(
        sum_a, sum_b, second1, second3, new_params, new_momentum
    )

    second2 = shift(second3, "y", -1)
    sum_a = exchange_sum(sum_a, ("xh", "y"))
    sum_a, first2, second2 = together(sum_a, first2, second2)

    grad_weight = jnp.concatenate([sum_a.T, sum_b.T], axis=-1) * factor

    me = lax.axis_index(GROUP)
    own_gain = lax.dynamic_slice_in_dim(norm_gain[0], me * rows, rows)
    own_sum = jnp.sum(own.astype(F32) * grad_weight, axis=-1) / own_gain
    place = jnp.stack([lax.axis_index(axis) for axis in GROUP])
    place = jnp.stack([lax.axis_index(axis) for axis in GROUP])
    grad_gain = lax.all_to_all(
        jnp.broadcast_to(own_sum[None], (devices, rows)), GROUP, 0, 0, tiled=True
    ).reshape(-1)
    vmem = pl.BlockSpec(memory_space=pltpu.VMEM)
    keys = cotangent.shape[1]
    tokens, features = hidden.shape
    operands = (place, hidden, norm_gain, cotangent, inverse)
    partial = rows_call(
        early_kernel,
        (0, 1, 3),
        (
            jax.ShapeDtypeStruct((tokens, features), F32),
            jax.ShapeDtypeStruct((tokens, keys), F32),
            jax.ShapeDtypeStruct((tokens, LANES), F32),
        ),
        (vmem,) * 3,
        (),
        operands,
        (first, second, first1, second1, first3, second3),
        "early_rows",
    )

    key_out, grad_hidden = rows_call(
        late_kernel,
        (2,),
        (
            jax.ShapeDtypeStruct((tokens, keys), BF16),
            jax.ShapeDtypeStruct((tokens, features), BF16),
        ),
        (vmem, pl.BlockSpec(memory_space=pl.ANY)),
        (
            pltpu.VMEM((tokens, keys), F32),
            pltpu.VMEM((tokens, LANES), F32),
            pltpu.VMEM((tokens, features // 4), F32),
            pltpu.VMEM((tokens, features), F32),
            pltpu.VMEM((4, tokens, features // 4), BF16),
            pltpu.SemaphoreType.DMA,
            pltpu.SemaphoreType.DMA((4,)),
        ),
        (*operands, *partial[1:], own_sum[None]),
        (partial[0], first2, second2),
        "late_rows",
    )

    return (
        key_out[None],
        grad_weight[None],
        grad_hidden[None],
        grad_gain[None],
        new_params,
        new_momentum,
    )


def solution(mesh):
    fine = Mesh(mesh.devices.reshape(2, 2, 2, 4, 8), (*REPL, *GROUP))
    placed = (
        P(REPL, GROUP, None),
        P(REPL, None),
        P(REPL, GROUP, None),
        P(REPL, GROUP, None),
        P(None, GROUP, None),
        P(None, GROUP, None),
        P(REPL, None, GROUP, None),
        P(),
    )
    return jax.shard_map(
        per_device,
        mesh=fine,
        in_specs=placed,
        out_specs=(
            P(REPL, GROUP, None),
            P(REPL, GROUP, None),
            P(REPL, GROUP, None),
            P(REPL, None),
            P(GROUP, None),
            P(GROUP, None),
        ),
        check_vma=False,
    )
```

```python
import functools

import jax
import jax.numpy as jnp
from jax import lax
from jax.experimental import pallas as pl
from jax.experimental.pallas import tpu as pltpu
from jax.sharding import Mesh
from jax.sharding import PartitionSpec as P

GROUP = ("xh", "y", "z")
REPL = ("xl", "core")
SIZE = {"xh": 2, "y": 4, "z": 8}
BF16 = jnp.bfloat16
F32 = jnp.float32
LANES = 128
ORDER = (0, 1, 7, 2, 6, 3, 5, 4)


def shift(value, axis, step):
    n = SIZE[axis]
    return lax.ppermute(value, axis, [(i, (i + step) % n) for i in range(n)])


def together(*values):
    return lax.optimization_barrier(values)


def term(part, axis, dim, step):
    at = (lax.axis_index(axis) + step) & (SIZE[axis] - 1)
    return lax.dynamic_slice_in_dim(part, at, 1, dim)


def added(part, axis, dim, step, received):
    mine = term(part, axis, dim, step).reshape(received.shape)
    return (mine.astype(F32) + received.astype(F32)).astype(BF16)


def exchange_sum(part, axes):
    blocks = lax.all_to_all(part.astype(BF16), axes, 0, 0, tiled=True)
    return jnp.sum(blocks.astype(F32), axis=0)


def weight_grad_kernel(hidden, gain, cotangent, a_out, b_out, inv_out, inverse, turned):
    step = pl.program_id(0)
    tokens, width = hidden.shape
    blocks, cut, _ = a_out.shape
    span = blocks * LANES

    @pl.when(step == 0)
    def _():
        def add(i, total):
            piece = hidden[:, pl.ds(pl.multiple_of(i * 512, 512), 512)].astype(F32)
            square = piece * piece
            for j in range(4):
                total = total + square[:, j * LANES : (j + 1) * LANES]
            return total

        total = lax.fori_loop(0, width // 512, add, jnp.zeros((tokens, LANES), F32))
        mean = jnp.sum(total, axis=-1, keepdims=True) / width
        inverse[...] = jnp.broadcast_to(lax.rsqrt(mean + 1e-05), (tokens, LANES))
        inv_out[...] = inverse[...]
        turned[...] = cotangent[...].T

    for j in range(0, blocks, 2):
        at = pl.ds(pl.multiple_of(step * span + j * LANES, 2 * LANES), 2 * LANES)
        scaled = (hidden[:, at].astype(F32) * inverse[:, :1] * gain[:, at]).astype(BF16)
        both = jnp.dot(turned[...], scaled, preferred_element_type=F32)
        for i in range(2):
            lanes = slice(i * LANES, (i + 1) * LANES)
            a_out[j + i] = both[:cut, lanes].astype(BF16)
            b_out[j + i] = both[cut:, lanes].astype(BF16)


def weight_grad(hidden, gain, cotangent):
    tokens, width = hidden.shape
    keys = cotangent.shape[1]
    blocks, per_step, cut = width // LANES, 8, keys // 2
    whole = lambda i: (0, 0)
    part = jax.ShapeDtypeStruct((blocks, cut, LANES), BF16)
    return pl.pallas_call(
        weight_grad_kernel,
        grid=(blocks // per_step,),
        out_shape=(part, part, jax.ShapeDtypeStruct((tokens, LANES), F32)),
        in_specs=[
            pl.BlockSpec((tokens, width), whole),
            pl.BlockSpec((1, width), whole),
            pl.BlockSpec((tokens, keys), whole),
        ],
        out_specs=(
            pl.BlockSpec((per_step, cut, LANES), lambda i: (i, 0, 0)),
            pl.BlockSpec((per_step, cut, LANES), lambda i: (i, 0, 0)),
            pl.BlockSpec((tokens, LANES), whole),
        ),
        scratch_shapes=[pltpu.VMEM((tokens, LANES), F32), pltpu.VMEM((keys, tokens), BF16)],
        compiler_params=pltpu.CompilerParams(vmem_limit_bytes=56 * 1024 * 1024),
        cost_estimate=pl.CostEstimate(
            flops=2 * tokens * width * keys, bytes_accessed=22 * 1024 * 1024, transcendentals=0
        ),
        name="weight_grad",
    )(hidden, gain, cotangent)


def use_blocks(steps, place, hidden, gain, cotangent, inverse, weights, held, sems, keys, dots, keep):
    x, y, z = place[0], place[1], place[2]
    split = weights[0].shape[1]
    places = (pl.ds(0, split), pl.ds(split, weights[1].shape[1]))
    for i, ref in enumerate(weights):
        for group in range(ref.shape[0]):
            lanes = pl.ds(group * LANES, LANES)
            there = held.at[i // 2, places[i % 2], lanes]
            pltpu.make_async_copy(ref.at[group], there, sems.at[i // 2]).start()

    def block(i, carry):
        index, half = i // 2, i % 2

        @pl.when(half == 0)
        def _():
            pltpu.make_async_copy(held.at[index], held.at[index], sems.at[index]).wait()

        yr = steps[0]
        for k in range(1, len(steps)):
            yr = jnp.where(index == k, steps[k], yr)
        rows = held[index, pl.ds(pl.multiple_of(half * 1024, 1024), 1024), :]
        grads = lax.dot_general(
            cotangent[...], rows, (((1,), (1,)), ((), ())), preferred_element_type=F32
        )
        scaled = []
        total = dots[...]
        for j in range(8):
            zr = jnp.where(half == 0, ORDER[j // 2], ORDER[4 + j // 2])
            near = x ^ (j % 2), (y - yr) & 3, (z - zr) & 7
            feature = near[0] * 32 + near[1] * 8 + near[2]
            at = pl.ds(pl.multiple_of(feature * LANES, LANES), LANES)
            normed = hidden[:, at].astype(F32) * inverse[...]
            weighted = grads[:, j * LANES : (j + 1) * LANES] * gain[:, at]
            keep(feature, near, weighted)
            total = total + weighted * normed
            scaled.append((normed * gain[:, at]).astype(BF16))
        dots[...] = total
        keys[...] += jnp.dot(
            jnp.concatenate(scaled, axis=1), rows, preferred_element_type=F32
        )
        return carry

    lax.fori_loop(0, 2 * len(steps), block, 0)


def early_kernel(steps, place, hidden, gain, cotangent, inverse, *refs):
    count = 2 * len(steps)
    grad, keys, dots, held, sems = refs[count:]
    keys[...] = jnp.zeros_like(keys)
    dots[...] = jnp.zeros_like(dots)

    def keep(feature, near, weighted):
        grad[:, pl.ds(pl.multiple_of(feature * LANES, LANES), LANES)] = weighted

    use_blocks(
        steps, place, hidden, gain, cotangent, inverse, refs[:count], held, sems, keys, dots, keep
    )


def late_kernel(steps, place, hidden, gain, cotangent, inverse, keys_in, dots_in, after, *refs):
    del after
    grad_hbm, weights = refs[0], refs[1 : 1 + 2 * len(steps)]
    outs = refs[1 + 2 * len(steps) :]
    key_out, grad_hidden, held, sems, keys, dots, fresh, grad, done, load_sem, store_sems = outs
    width = hidden.shape[1]
    load = pltpu.make_async_copy(grad_hbm, grad, load_sem)
    load.start()
    keys[...] = keys_in[...]
    dots[...] = dots_in[...]

    def keep(feature, near, weighted):
        at = (near[0] * 8 + near[2]) * LANES
        fresh[:, pl.ds(pl.multiple_of(at, LANES), LANES)] = weighted

    use_blocks(
        steps, place, hidden, gain, cotangent, inverse, weights, held, sems, keys, dots, keep
    )
    key_out[...] = keys[...].astype(BF16)
    mean = jnp.sum(dots[...], axis=-1, keepdims=True) / width
    inv = inverse[:, :1]
    y = (place[1] - steps[0]) & 3
    load.wait()

    stores = []
    for quarter in range(4):

        def finish(i, carry, quarter=quarter):
            part = quarter * 4 + i
            at = pl.ds(pl.multiple_of(part * 512, 512), 512)
            here = (part // 8) * 1024 + (part % 2) * 512
            new = fresh[:, pl.ds(pl.multiple_of(here, 512), 512)]
            weighted = jnp.where((part // 2) % 4 == y, new, grad[:, at])
            normed = hidden[:, at].astype(F32) * inv
            lanes = pl.ds(pl.multiple_of(i * 512, 512), 512)
            done[quarter, :, lanes] = (inv * (weighted - normed * mean)).astype(BF16)
            return carry

        lax.fori_loop(0, 4, finish, 0)
        there = grad_hidden.at[:, pl.ds(quarter * 2048, 2048)]
        stores.append(pltpu.make_async_copy(done.at[quarter], there, store_sems.at[quarter]))
        stores[-1].start()
    for store in stores:
        store.wait()


def rows_call(kernel, steps, outs, out_specs, scratch, operands, weights, name):
    hidden, cotangent = operands[1], operands[3]
    tokens, width = hidden.shape
    keys = cotangent.shape[1]
    vmem = pl.BlockSpec(memory_space=pltpu.VMEM)
    return pl.pallas_call(
        functools.partial(kernel, steps),
        out_shape=outs,
        in_specs=[pl.BlockSpec(memory_space=pltpu.SMEM)]
        + [vmem] * (len(operands) - 1)
        + [pl.BlockSpec(memory_space=pl.ANY)] * len(weights),
        out_specs=out_specs,
        scratch_shapes=[
            pltpu.VMEM((len(steps), width // 4, keys), BF16),
            pltpu.SemaphoreType.DMA((len(steps),)),
            *scratch,
        ],
        compiler_params=pltpu.CompilerParams(vmem_limit_bytes=60 * 1024 * 1024),
        cost_estimate=pl.CostEstimate(
            flops=len(steps) * tokens * width * keys,
            bytes_accessed=(12 + 2 * len(steps)) * 1024 * 1024,
            transcendentals=0,
        ),
        name=name,
    )(*operands, *weights)


def outer_step(current, moment, average):
    moment_new = 0.9 * moment + average
    return (current - 0.7 * (average + 0.9 * moment_new), moment_new)


def per_device(
    hidden_in,
    norm_gain,
    key_weight,
    key_cotangent,
    outer_params,
    outer_momentum,
    inner_params,
    fragment_index,
):
    hidden = hidden_in[0]
    cotangent = key_cotangent[0]
    own = key_weight[0]
    rows, width = own.shape
    cut = width // 2
    groups = SIZE["xh"], SIZE["y"], SIZE["z"]
    devices = groups[0] * groups[1] * groups[2]
    factor = float(hidden.shape[0] * devices) ** (-0.5)

    chosen = fragment_index[0]
    current = lax.dynamic_index_in_dim(outer_params, chosen, 0, keepdims=False)
    inner_now = lax.dynamic_index_in_dim(inner_params[0], chosen, 0, keepdims=False)
    part_a, part_b, inverse = weight_grad(hidden, norm_gain, cotangent)
    part_a = part_a.reshape(*groups, cut, rows)
    part_b = part_b.reshape(*groups, cut, rows)
    half = cut // 2

    mine = current - inner_now
    slabs = own.reshape(rows, -1, LANES).transpose(1, 0, 2)
    over_x = shift(slabs, "xh", 1)
    core = lax.ppermute(mine, "core", [(0, 1), (1, 0)])
    over_x, part_a, part_b, inverse, core = together(over_x, part_a, part_b, inverse, core)
    pair = jnp.concatenate([slabs, over_x], axis=1)

    sums = groups[0] * groups[1]

    def along_z(total, slab, step):
        return shift(jnp.concatenate([total.reshape(sums, cut, rows), slab]), "z", step)

    far_b = term(part_b, "y", 1, 2)
    left = along_z(term(part_a, "z", 2, -4), pair, -1)
    right = along_z(term(part_a, "z", 2, 3), pair, 1)
    b_left = shift(far_b[..., half:, :], "y", -1)
    b_right = shift(far_b[..., :half, :], "y", 1)
    left, right, b_left, b_right = together(left, right, b_left, b_right)

    z7, z1 = left[sums:], right[sums:]
    left = along_z(added(part_a, "z", 2, -3, left[:sums]), z7, -1)
    right = along_z(added(part_a, "z", 2, 2, right[:sums]), z1, 1)
    none = jnp.zeros_like(b_left)
    b_left = shift(
        added(part_b, "y", 1, -1, jnp.concatenate([none, b_left], axis=3)), "y", -1
    )
    b_right = shift(
        added(part_b, "y", 1, 1, jnp.concatenate([b_right, none], axis=3)), "y", 1
    )
    left, right, b_left, b_right = together(left, right, b_left, b_right)

    z6, z2 = left[sums:], right[sums:]
    left = along_z(added(part_a, "z", 2, -2, left[:sums]), z6, -1)
    right = along_z(added(part_a, "z", 2, 1, right[:sums]), z2, 1)
    first = jnp.concatenate([pair, z1, z7, z2, z6], axis=1)
    first1, first3 = shift(first, "y", 1), shift(first, "y", -1)
    left, right = together(left, right)

    z5, z3 = left[sums:], right[sums:]
    left = shift(added(part_a, "z", 2, -1, left[:sums]), "z", -1)
    z4 = shift(z3, "z", 1)
    left, right, z4, first1, first3, b_left, b_right, core = together(
        left, right, z4, first1, first3, b_left, b_right, core
    )

    second = jnp.concatenate([z3, z5, z4], axis=1)
    second1, second3 = shift(second, "y", 1), shift(second, "y", -1)
    sum_a = term(part_a, "z", 2, 0).reshape(left.shape).astype(F32)
    sum_a = sum_a + left.astype(F32) + right[:sums].astype(F32)
    sum_a = exchange_sum(sum_a.reshape(-1, cut, rows), ("xh", "y"))
    sum_b = term(part_b, "y", 1, 0).astype(F32) + b_left.astype(F32) + b_right.astype(F32)
    at_x = lax.axis_index("xh")
    away = lax.dynamic_slice_in_dim(sum_b, 1 - at_x, 1, 0).astype(BF16)
    sum_b = lax.dynamic_slice_in_dim(sum_b, at_x, 1, 0) + shift(away, "xh", 1).astype(F32)
    sum_b = sum_b.reshape(-1, cut, rows).astype(BF16)
    both = mine + core
    summed = both + lax.ppermute(both, "xl", [(0, 1), (1, 0)])
    moment = lax.dynamic_index_in_dim(outer_momentum, chosen, 0, keepdims=False)
    new_params, new_momentum = outer_step(current, moment, summed / 4.0)
    first2 = shift(first1, "y", 1)
    sum_a, sum_b, second1, second3, new_params, new_momentum = together(
        sum_a, sum_b, second1, second3, new_params, new_momentum
    )

    second2 = shift(second3, "y", -1)
    sum_b = exchange_sum(sum_b, "z")

    grad_weight = jnp.concatenate([sum_a.T, sum_b.T], axis=-1) * factor

    me = lax.axis_index(GROUP)
    own_gain = lax.dynamic_slice_in_dim(norm_gain[0], me * rows, rows)
    own_sum = jnp.sum(own.astype(F32) * grad_weight, axis=-1) / own_gain
    place = jnp.stack([lax.axis_index(axis) for axis in GROUP])
    place = jnp.stack([lax.axis_index(axis) for axis in GROUP])
    grad_gain = lax.all_to_all(
        jnp.broadcast_to(own_sum[None], (devices, rows)), GROUP, 0, 0, tiled=True
    ).reshape(-1)
    vmem = pl.BlockSpec(memory_space=pltpu.VMEM)
    keys = cotangent.shape[1]
    tokens, features = hidden.shape
    operands = (place, hidden, norm_gain, cotangent, inverse)
    partial = rows_call(
        early_kernel,
        (0, 1, 3),
        (
            jax.ShapeDtypeStruct((tokens, features), F32),
            jax.ShapeDtypeStruct((tokens, keys), F32),
            jax.ShapeDtypeStruct((tokens, LANES), F32),
        ),
        (vmem,) * 3,
        (),
        operands,
        (first, second, first1, second1, first3, second3),
        "early_rows",
    )

    key_out, grad_hidden = rows_call(
        late_kernel,
        (2,),
        (
            jax.ShapeDtypeStruct((tokens, keys), BF16),
            jax.ShapeDtypeStruct((tokens, features), BF16),
        ),
        (vmem, pl.BlockSpec(memory_space=pl.ANY)),
        (
            pltpu.VMEM((tokens, keys), F32),
            pltpu.VMEM((tokens, LANES), F32),
            pltpu.VMEM((tokens, features // 4), F32),
            pltpu.VMEM((tokens, features), F32),
            pltpu.VMEM((4, tokens, features // 4), BF16),
            pltpu.SemaphoreType.DMA,
            pltpu.SemaphoreType.DMA((4,)),
        ),
        (*operands, *partial[1:], own_sum[None]),
        (partial[0], first2, second2),
        "late_rows",
    )

    return (
        key_out[None],
        grad_weight[None],
        grad_hidden[None],
        grad_gain[None],
        new_params,
        new_momentum,
    )


def solution(mesh):
    fine = Mesh(mesh.devices.reshape(2, 2, 2, 4, 8), (*REPL, *GROUP))
    placed = (
        P(REPL, GROUP, None),
        P(REPL, None),
        P(REPL, GROUP, None),
        P(REPL, GROUP, None),
        P(None, GROUP, None),
        P(None, GROUP, None),
        P(REPL, None, GROUP, None),
        P(),
    )
    return jax.shard_map(
        per_device,
        mesh=fine,
        in_specs=placed,
        out_specs=(
            P(REPL, GROUP, None),
            P(REPL, GROUP, None),
            P(REPL, GROUP, None),
            P(REPL, None),
            P(GROUP, None),
            P(GROUP, None),
        ),
        check_vma=False,
    )
```

```python
import functools

import jax
import jax.numpy as jnp
from jax import lax
from jax.experimental import pallas as pl
from jax.experimental.pallas import tpu as pltpu
from jax.sharding import Mesh
from jax.sharding import PartitionSpec as P

GROUP = ("xh", "y", "z")
REPL = ("xl", "core")
SIZE = {"xh": 2, "y": 4, "z": 8}
BF16 = jnp.bfloat16
F32 = jnp.float32
LANES = 128
ORDER = (0, 1, 7, 2, 6, 3, 5, 4)


def shift(value, axis, step):
    n = SIZE[axis]
    return lax.ppermute(value, axis, [(i, (i + step) % n) for i in range(n)])


def together(*values):
    return lax.optimization_barrier(values)


def term(part, axis, dim, step):
    at = (lax.axis_index(axis) + step) & (SIZE[axis] - 1)
    return lax.dynamic_slice_in_dim(part, at, 1, dim)


def added(part, axis, dim, step, received):
    mine = term(part, axis, dim, step).reshape(received.shape)
    return (mine.astype(F32) + received.astype(F32)).astype(BF16)


def exchange_sum(part, axes):
    blocks = lax.all_to_all(part.astype(BF16), axes, 0, 0, tiled=True)
    return jnp.sum(blocks.astype(F32), axis=0)


def weight_grad_kernel(hidden, gain, cotangent, a_out, b_out, inv_out, inverse, turned):
    step = pl.program_id(0)
    tokens, width = hidden.shape
    blocks, cut, _ = a_out.shape
    span = blocks * LANES

    @pl.when(step == 0)
    def _():
        def add(i, total):
            piece = hidden[:, pl.ds(pl.multiple_of(i * 512, 512), 512)].astype(F32)
            square = piece * piece
            for j in range(4):
                total = total + square[:, j * LANES : (j + 1) * LANES]
            return total

        total = lax.fori_loop(0, width // 512, add, jnp.zeros((tokens, LANES), F32))
        mean = jnp.sum(total, axis=-1, keepdims=True) / width
        inverse[...] = jnp.broadcast_to(lax.rsqrt(mean + 1e-05), (tokens, LANES))
        inv_out[...] = inverse[...]
        turned[...] = cotangent[...].T

    for j in range(0, blocks, 2):
        at = pl.ds(pl.multiple_of(step * span + j * LANES, 2 * LANES), 2 * LANES)
        scaled = (hidden[:, at].astype(F32) * inverse[:, :1] * gain[:, at]).astype(BF16)
        both = jnp.dot(turned[...], scaled, preferred_element_type=F32)
        for i in range(2):
            lanes = slice(i * LANES, (i + 1) * LANES)
            a_out[j + i] = both[:cut, lanes].astype(BF16)
            b_out[j + i] = both[cut:, lanes].astype(BF16)


def weight_grad(hidden, gain, cotangent):
    tokens, width = hidden.shape
    keys = cotangent.shape[1]
    blocks, per_step, cut = width // LANES, 8, keys // 2
    whole = lambda i: (0, 0)
    part = jax.ShapeDtypeStruct((blocks, cut, LANES), BF16)
    return pl.pallas_call(
        weight_grad_kernel,
        grid=(blocks // per_step,),
        out_shape=(part, part, jax.ShapeDtypeStruct((tokens, LANES), F32)),
        in_specs=[
            pl.BlockSpec((tokens, width), whole),
            pl.BlockSpec((1, width), whole),
            pl.BlockSpec((tokens, keys), whole),
        ],
        out_specs=(
            pl.BlockSpec((per_step, cut, LANES), lambda i: (i, 0, 0)),
            pl.BlockSpec((per_step, cut, LANES), lambda i: (i, 0, 0)),
            pl.BlockSpec((tokens, LANES), whole),
        ),
        scratch_shapes=[pltpu.VMEM((tokens, LANES), F32), pltpu.VMEM((keys, tokens), BF16)],
        compiler_params=pltpu.CompilerParams(vmem_limit_bytes=56 * 1024 * 1024),
        cost_estimate=pl.CostEstimate(
            flops=2 * tokens * width * keys, bytes_accessed=22 * 1024 * 1024, transcendentals=0
        ),
        name="weight_grad",
    )(hidden, gain, cotangent)


def use_blocks(steps, place, hidden, gain, cotangent, inverse, weights, held, sems, keys, dots, keep):
    x, y, z = place[0], place[1], place[2]
    split = weights[0].shape[1]
    places = (pl.ds(0, split), pl.ds(split, weights[1].shape[1]))
    for i, ref in enumerate(weights):
        for group in range(ref.shape[0]):
            lanes = pl.ds(group * LANES, LANES)
            there = held.at[i // 2, places[i % 2], lanes]
            pltpu.make_async_copy(ref.at[group], there, sems.at[i // 2]).start()

    def block(i, carry):
        index, half = i // 2, i % 2

        @pl.when(half == 0)
        def _():
            pltpu.make_async_copy(held.at[index], held.at[index], sems.at[index]).wait()

        yr = steps[0]
        for k in range(1, len(steps)):
            yr = jnp.where(index == k, steps[k], yr)
        rows = held[index, pl.ds(pl.multiple_of(half * 1024, 1024), 1024), :]
        grads = lax.dot_general(
            cotangent[...], rows, (((1,), (1,)), ((), ())), preferred_element_type=F32
        )
        scaled = []
        total = dots[...]
        for j in range(8):
            zr = jnp.where(half == 0, ORDER[j // 2], ORDER[4 + j // 2])
            near = x ^ (j % 2), (y - yr) & 3, (z - zr) & 7
            feature = near[0] * 32 + near[1] * 8 + near[2]
            at = pl.ds(pl.multiple_of(feature * LANES, LANES), LANES)
            normed = hidden[:, at].astype(F32) * inverse[...]
            weighted = grads[:, j * LANES : (j + 1) * LANES] * gain[:, at]
            keep(feature, near, weighted)
            total = total + weighted * normed
            scaled.append((normed * gain[:, at]).astype(BF16))
        dots[...] = total
        keys[...] += jnp.dot(
            jnp.concatenate(scaled, axis=1), rows, preferred_element_type=F32
        )
        return carry

    lax.fori_loop(0, 2 * len(steps), block, 0)


def early_kernel(steps, place, hidden, gain, cotangent, inverse, *refs):
    count = 2 * len(steps)
    grad, keys, dots, held, sems = refs[count:]
    keys[...] = jnp.zeros_like(keys)
    dots[...] = jnp.zeros_like(dots)

    def keep(feature, near, weighted):
        grad[:, pl.ds(pl.multiple_of(feature * LANES, LANES), LANES)] = weighted

    use_blocks(
        steps, place, hidden, gain, cotangent, inverse, refs[:count], held, sems, keys, dots, keep
    )


def late_kernel(steps, place, hidden, gain, cotangent, inverse, keys_in, dots_in, after, *refs):
    del after
    grad_hbm, weights = refs[0], refs[1 : 1 + 2 * len(steps)]
    outs = refs[1 + 2 * len(steps) :]
    key_out, grad_hidden, held, sems, keys, dots, fresh, grad, done, load_sem, store_sems = outs
    width = hidden.shape[1]
    load = pltpu.make_async_copy(grad_hbm, grad, load_sem)
    load.start()
    keys[...] = keys_in[...]
    dots[...] = dots_in[...]

    def keep(feature, near, weighted):
        at = (near[0] * 8 + near[2]) * LANES
        fresh[:, pl.ds(pl.multiple_of(at, LANES), LANES)] = weighted

    use_blocks(
        steps, place, hidden, gain, cotangent, inverse, weights, held, sems, keys, dots, keep
    )
    key_out[...] = keys[...].astype(BF16)
    mean = jnp.sum(dots[...], axis=-1, keepdims=True) / width
    inv = inverse[:, :1]
    y = (place[1] - steps[0]) & 3
    load.wait()

    stores = []
    for quarter in range(4):

        def finish(i, carry, quarter=quarter):
            part = quarter * 4 + i
            at = pl.ds(pl.multiple_of(part * 512, 512), 512)
            here = (part // 8) * 1024 + (part % 2) * 512
            new = fresh[:, pl.ds(pl.multiple_of(here, 512), 512)]
            weighted = jnp.where((part // 2) % 4 == y, new, grad[:, at])
            normed = hidden[:, at].astype(F32) * inv
            lanes = pl.ds(pl.multiple_of(i * 512, 512), 512)
            done[quarter, :, lanes] = (inv * (weighted - normed * mean)).astype(BF16)
            return carry

        lax.fori_loop(0, 4, finish, 0)
        there = grad_hidden.at[:, pl.ds(quarter * 2048, 2048)]
        stores.append(pltpu.make_async_copy(done.at[quarter], there, store_sems.at[quarter]))
        stores[-1].start()
    for store in stores:
        store.wait()


def rows_call(kernel, steps, outs, out_specs, scratch, operands, weights, name):
    hidden, cotangent = operands[1], operands[3]
    tokens, width = hidden.shape
    keys = cotangent.shape[1]
    vmem = pl.BlockSpec(memory_space=pltpu.VMEM)
    return pl.pallas_call(
        functools.partial(kernel, steps),
        out_shape=outs,
        in_specs=[pl.BlockSpec(memory_space=pltpu.SMEM)]
        + [vmem] * (len(operands) - 1)
        + [pl.BlockSpec(memory_space=pl.ANY)] * len(weights),
        out_specs=out_specs,
        scratch_shapes=[
            pltpu.VMEM((len(steps), width // 4, keys), BF16),
            pltpu.SemaphoreType.DMA((len(steps),)),
            *scratch,
        ],
        compiler_params=pltpu.CompilerParams(vmem_limit_bytes=60 * 1024 * 1024),
        cost_estimate=pl.CostEstimate(
            flops=len(steps) * tokens * width * keys,
            bytes_accessed=(12 + 2 * len(steps)) * 1024 * 1024,
            transcendentals=0,
        ),
        name=name,
    )(*operands, *weights)


def outer_step(current, moment, average):
    moment_new = 0.9 * moment + average
    return (current - 0.7 * (average + 0.9 * moment_new), moment_new)


def per_device(
    hidden_in,
    norm_gain,
    key_weight,
    key_cotangent,
    outer_params,
    outer_momentum,
    inner_params,
    fragment_index,
):
    hidden = hidden_in[0]
    cotangent = key_cotangent[0]
    own = key_weight[0]
    rows, width = own.shape
    cut = width // 2
    groups = SIZE["xh"], SIZE["y"], SIZE["z"]
    devices = groups[0] * groups[1] * groups[2]
    factor = float(hidden.shape[0] * devices) ** (-0.5)

    chosen = fragment_index[0]
    current = lax.dynamic_index_in_dim(outer_params, chosen, 0, keepdims=False)
    inner_now = lax.dynamic_index_in_dim(inner_params[0], chosen, 0, keepdims=False)
    part_a, part_b, inverse = weight_grad(hidden, norm_gain, cotangent)
    part_a = part_a.reshape(*groups, cut, rows)
    part_b = part_b.reshape(*groups, cut, rows)
    half = cut // 2

    mine = current - inner_now
    slabs = own.reshape(rows, -1, LANES).transpose(1, 0, 2)
    over_x = shift(slabs, "xh", 1)
    core = lax.ppermute(mine, "core", [(0, 1), (1, 0)])
    over_x, part_a, part_b, inverse, core = together(over_x, part_a, part_b, inverse, core)
    pair = jnp.concatenate([slabs, over_x], axis=1)

    sums = groups[0] * groups[1]

    def along_z(total, slab, step):
        return shift(jnp.concatenate([total.reshape(sums, cut, rows), slab]), "z", step)

    far_b = term(part_b, "y", 1, 2)
    left = along_z(term(part_a, "z", 2, -4), pair, -1)
    right = along_z(term(part_a, "z", 2, 3), pair, 1)
    b_left = shift(far_b[..., half:, :], "y", -1)
    b_right = shift(far_b[..., :half, :], "y", 1)
    left, right, b_left, b_right = together(left, right, b_left, b_right)

    z7, z1 = left[sums:], right[sums:]
    left = along_z(added(part_a, "z", 2, -3, left[:sums]), z7, -1)
    right = along_z(added(part_a, "z", 2, 2, right[:sums]), z1, 1)
    none = jnp.zeros_like(b_left)
    b_left = shift(
        added(part_b, "y", 1, -1, jnp.concatenate([none, b_left], axis=3)), "y", -1
    )
    b_right = shift(
        added(part_b, "y", 1, 1, jnp.concatenate([b_right, none], axis=3)), "y", 1
    )
    left, right, b_left, b_right = together(left, right, b_left, b_right)

    z6, z2 = left[sums:], right[sums:]
    left = along_z(added(part_a, "z", 2, -2, left[:sums]), z6, -1)
    right = along_z(added(part_a, "z", 2, 1, right[:sums]), z2, 1)
    first = jnp.concatenate([pair, z1, z7, z2, z6], axis=1)
    first1, first3 = shift(first, "y", 1), shift(first, "y", -1)
    left, right = together(left, right)

    z5, z3 = left[sums:], right[sums:]
    left = shift(added(part_a, "z", 2, -1, left[:sums]), "z", -1)
    z4 = shift(z3, "z", 1)
    sum_b = term(part_b, "y", 1, 0).astype(F32) + b_left.astype(F32) + b_right.astype(F32)
    at_x = lax.axis_index("xh")
    over_x = shift(lax.dynamic_slice_in_dim(sum_b, 1 - at_x, 1, 0).astype(BF16), "xh", 1)
    sum_b = lax.dynamic_slice_in_dim(sum_b, at_x, 1, 0) + over_x.astype(F32)
    sum_b = sum_b.reshape(-1, cut, rows).astype(BF16)
    left, right, z4, first1, first3, sum_b, core = together(
        left, right, z4, first1, first3, sum_b, core
    )

    second = jnp.concatenate([z3, z5, z4], axis=1)
    second1, second3 = shift(second, "y", 1), shift(second, "y", -1)
    sum_a = term(part_a, "z", 2, 0).reshape(left.shape).astype(F32)
    sum_a = sum_a + left.astype(F32) + right[:sums].astype(F32)
    sum_a = exchange_sum(sum_a.reshape(-1, cut, rows), ("xh", "y"))
    both = mine + core
    summed = both + lax.ppermute(both, "xl", [(0, 1), (1, 0)])
    moment = lax.dynamic_index_in_dim(outer_momentum, chosen, 0, keepdims=False)
    new_params, new_momentum = outer_step(current, moment, summed / 4.0)
    first2 = shift(first1, "y", 1)
    sum_a, sum_b, second1, second3, new_params, new_momentum = together(
        sum_a, sum_b, second1, second3, new_params, new_momentum
    )

    second2 = shift(second3, "y", -1)
    sum_b = exchange_sum(sum_b, "z")

    grad_weight = jnp.concatenate([sum_a.T, sum_b.T], axis=-1) * factor

    me = lax.axis_index(GROUP)
    own_gain = lax.dynamic_slice_in_dim(norm_gain[0], me * rows, rows)
    own_sum = jnp.sum(own.astype(F32) * grad_weight, axis=-1) / own_gain
    place = jnp.stack([lax.axis_index(axis) for axis in GROUP])
    place = jnp.stack([lax.axis_index(axis) for axis in GROUP])
    grad_gain = lax.all_to_all(
        jnp.broadcast_to(own_sum[None], (devices, rows)), GROUP, 0, 0, tiled=True
    ).reshape(-1)
    vmem = pl.BlockSpec(memory_space=pltpu.VMEM)
    keys = cotangent.shape[1]
    tokens, features = hidden.shape
    operands = (place, hidden, norm_gain, cotangent, inverse)
    partial = rows_call(
        early_kernel,
        (0, 1, 3),
        (
            jax.ShapeDtypeStruct((tokens, features), F32),
            jax.ShapeDtypeStruct((tokens, keys), F32),
            jax.ShapeDtypeStruct((tokens, LANES), F32),
        ),
        (vmem,) * 3,
        (),
        operands,
        (first, second, first1, second1, first3, second3),
        "early_rows",
    )

    key_out, grad_hidden = rows_call(
        late_kernel,
        (2,),
        (
            jax.ShapeDtypeStruct((tokens, keys), BF16),
            jax.ShapeDtypeStruct((tokens, features), BF16),
        ),
        (vmem, pl.BlockSpec(memory_space=pl.ANY)),
        (
            pltpu.VMEM((tokens, keys), F32),
            pltpu.VMEM((tokens, LANES), F32),
            pltpu.VMEM((tokens, features // 4), F32),
            pltpu.VMEM((tokens, features), F32),
            pltpu.VMEM((4, tokens, features // 4), BF16),
            pltpu.SemaphoreType.DMA,
            pltpu.SemaphoreType.DMA((4,)),
        ),
        (*operands, *partial[1:], own_sum[None]),
        (partial[0], first2, second2),
        "late_rows",
    )

    return (
        key_out[None],
        grad_weight[None],
        grad_hidden[None],
        grad_gain[None],
        new_params,
        new_momentum,
    )


def solution(mesh):
    fine = Mesh(mesh.devices.reshape(2, 2, 2, 4, 8), (*REPL, *GROUP))
    placed = (
        P(REPL, GROUP, None),
        P(REPL, None),
        P(REPL, GROUP, None),
        P(REPL, GROUP, None),
        P(None, GROUP, None),
        P(None, GROUP, None),
        P(REPL, None, GROUP, None),
        P(),
    )
    return jax.shard_map(
        per_device,
        mesh=fine,
        in_specs=placed,
        out_specs=(
            P(REPL, GROUP, None),
            P(REPL, GROUP, None),
            P(REPL, GROUP, None),
            P(REPL, None),
            P(GROUP, None),
            P(GROUP, None),
        ),
        check_vma=False,
    )
```
